32 devices in a mesh: section: 2 (over x), patch: 4 (over y, core), shard: 4 (over z).
Axes of the slice: x: 2, y: 2, z: 4, core: 2. Of those that a mesh axis runs over, the one named last changes fastest.
Arguments:
- hidden: bfloat16 [8, 1024, 2432], P('shard', 'patch'), may hold values from -6 to 6
- text_kv: bfloat16 [2, 8, 154, 2432], P('section', 'shard'), may hold values from -6 to 6, as said below
- stale_kv: bfloat16 [2, 8, 1024, 2432], P('section', 'shard', 'patch'), may hold values from -6 to 6, as said below
- modulation: float32 [2, 8, 3, 2432], P('section', 'shard'), may hold values from -3 to 3
- score_gain: float32 [2, 64], P('section'), may hold values from 1.5 to 4
- qkv_weight: bfloat16 [2, 2432, 3648], P('section', 'shard'), may hold values from -0.125 to 0.125
- out_weight: bfloat16 [2, 1216, 2432], P('section', None, 'shard'), may hold values from -0.15625 to 0.15625
- final_mod: float32 [8, 2, 2432], P('shard'), may hold values from -3 to 3
- final_weight: bfloat16 [2432, 64], replicated, may hold values from -0.125 to 0.125
- latent: float32 [8, 1024, 64], P('shard', ('patch', 'section')), may hold values from -6 to 6
- step_index: int32 [8], P('shard'), may hold values from 0 to 27
Outputs:
- new_kv: bfloat16 [2, 8, 1024, 2432], P('section', 'shard', 'patch')
- latent_next: float32 [8, 1024, 64], P('shard', ('patch', 'section'))
- denoised: float32 [8, 1024, 64], P('shard', ('patch', 'section'))
The draws below stay inside these ranges and needn't reach their ends.
Inputs may be any that keep to these rules, and one draw needn't show every extreme that they name: `text_kv`: in every row the first 1216 columns are 19 heads of 64 key features, each head with mean square one up to bfloat16 rounding. `stale_kv`: in every row the first 1216 columns are 19 heads of 64 key features, each head with mean square one up to bfloat16 rounding.
All inputs are finite; a program needn't handle non-finite values.
Results may differ from the reference program's by a relative error of at most 0.008.
Values may be sent and summed in bfloat16 or wider, within the bound.
A program may use at most 192 MiB of HBM per device.

```python
import math
import jax
import jax.numpy as jnp
from jax import lax

D = 2432
HEADS = 19
HEAD = 64
IMG = 1024
TXT = 154
CH = 64
NSTEPS = 28
HW = 1216
QKV = 3648
IMG_DEV = 256
REQ = 8
LAYERS = 2
N_PATCH = 4


def keys_values(key, rows, salt):
    key = jax.random.fold_in(key, salt)
    key_angle, key_value = jax.random.split(key, 2)
    half = HEAD // 2
    angle = jax.random.uniform(key_angle, (LAYERS, REQ, rows, HEADS, half), jnp.float32, -math.pi, math.pi)
    keys = jnp.concatenate([jnp.cos(angle), jnp.sin(angle)], -1) * math.sqrt(2.0)
    keys = keys.reshape(LAYERS, REQ, rows, HW)
    values = jnp.clip(jax.random.normal(key_value, (LAYERS, REQ, rows, HW), jnp.float32), -6.0, 6.0)
    return jnp.concatenate([keys, values], -1).astype(jnp.bfloat16)


def draw_text_kv(key, part):
    return keys_values(key, TXT, 101)


def draw_stale_kv(key, part):
    return keys_values(key, IMG, 202)


def plant(array, stream_key, least, top_value):
    longest = array.shape.index(max(array.shape))
    spots = []
    for shift in (0, 1):
        where = [jax.random.randint(jax.random.fold_in(stream_key, axis), (), 0, length) for axis, length in enumerate(array.shape)]
        where[longest] = (where[longest] + shift) % array.shape[longest]
        spots.append(tuple(where))
    return array.at[spots[0]].set(least).at[spots[1]].set(top_value)


def shard_levels(own_key, shape, shards, least, high):
    factor_of = 1.0
    for dim, parts in shards:
        heights = jax.random.uniform(jax.random.fold_in(jax.random.fold_in(own_key, 6), dim), (parts,), jnp.float32, least / len(shards), high / len(shards))
        factor_of = factor_of * jnp.repeat(jnp.exp(heights), shape[dim] // parts).reshape((-1,) + (1,) * (len(shape) - 1 - dim))
    return factor_of


def gaussian(own_key, shape, spread, reach, cuts=(), held_as=jnp.bfloat16):
    array = jax.random.normal(own_key, shape, jnp.float32) * spread
    if len(cuts) > 0:
        array = shard_levels(own_key, shape, cuts, -0.22, 0.18) * array
    return jnp.clip(array, min=-reach, max=reach).astype(held_as)


def setup_inputs(seed: int = 0) -> dict:
    seeds = jax.random.split(jax.random.key(seed), 12)
    return {
        "hidden": gaussian(seeds[0], (REQ, IMG, D), 1.0, 6.0, ((0, 4), (1, 4))),
        "text_kv": draw_text_kv(jax.random.fold_in(seeds[11], 71), 0),
        "stale_kv": draw_stale_kv(jax.random.fold_in(seeds[11], 71), 0),
        "modulation": gaussian(seeds[3], (LAYERS, REQ, 3, D), 0.6, 3.0, ((0, 2), (1, 4)), jnp.float32),
        "score_gain": jnp.clip(jnp.exp(math.log(4.0) - 0.98082925 * jax.random.uniform(seeds[4], (LAYERS, HEAD), jnp.float32) ** shard_levels(seeds[4], (LAYERS, HEAD), ((0, 2),), -0.2, 0.2)), 1.5, 4.0),
        "qkv_weight": gaussian(seeds[5], (LAYERS, D, QKV), D ** -0.5, 0.125, ((0, 2), (1, 4))),
        "out_weight": gaussian(seeds[6], (LAYERS, HW, D), HW ** -0.5, 0.15625, ((0, 2), (2, 4))),
        "final_mod": gaussian(seeds[7], (REQ, 2, D), 0.5, 3.0, ((0, 4),), jnp.float32),
        "final_weight": gaussian(seeds[8], (D, CH), D ** -0.5, 0.125),
        "latent": gaussian(seeds[9], (REQ, IMG, CH), 1.0, 6.0, ((0, 4), (1, 8)), jnp.float32),
        "step_index": plant(jax.random.randint(seeds[10], (REQ,), 0, NSTEPS), jax.random.fold_in(seeds[10], 1), 0, NSTEPS - 1).astype(jnp.int32),
    }


eps_norm = 1e-06
flow_shift = 3.0

def sigma_of(step):
    s = 1.0 - step.astype(jnp.float32) / NSTEPS
    return flow_shift * s / (1.0 + (flow_shift - 1.0) * s)

def modulated(xf, shift, scale):
    mean = lax.optimization_barrier(jnp.mean(xf, -1, keepdims=True))
    cent = xf - mean
    var = lax.optimization_barrier(jnp.mean(cent * cent, -1, keepdims=True))
    return cent * lax.rsqrt(var + eps_norm) * (1.0 + scale) + shift

def attend(query, keys_all):
    count = keys_all.shape[0]
    keys = keys_all[:, :HW].reshape(count, HEADS, HEAD).astype(jnp.float32)
    values = keys_all[:, HW:].reshape(count, HEADS, HEAD).astype(jnp.float32)
    scores = jnp.einsum('qhe,khe->hqk', query.astype(jnp.float32), keys)
    expo = jnp.exp(scores)
    total = lax.optimization_barrier(jnp.sum(expo, -1))
    weights = expo.astype(jnp.bfloat16)
    mixed = jnp.einsum('hqk,khe->qhe', weights.astype(jnp.float32), values)
    mixed = mixed / jnp.transpose(total)[:, :, None]
    return mixed.reshape(query.shape[0], HW).astype(jnp.bfloat16)

def reference(hidden, text_kv, stale_kv, modulation, score_gain, qkv_weight, out_weight, final_mod, final_weight, latent, step_index):

    def one_request(items):
        x, text_r, stale_r, mod_r, fmod, lat, step = items
        fresh_list = []
        for layer in range(LAYERS):
            xf = x.astype(jnp.float32)
            normed = modulated(xf, mod_r[layer, 0], mod_r[layer, 1]).astype(jnp.bfloat16)
            proj_in = jnp.dot(normed, qkv_weight[layer], preferred_element_type=jnp.float32)
            q = proj_in[:, :HW].reshape(IMG, HEADS, HEAD)
            k = proj_in[:, HW:2 * HW].reshape(IMG, HEADS, HEAD)
            v = proj_in[:, 2 * HW:]
            q_hat = q * lax.rsqrt(lax.optimization_barrier(jnp.mean(q * q, -1, keepdims=True)) + eps_norm)
            k_hat = k * lax.rsqrt(lax.optimization_barrier(jnp.mean(k * k, -1, keepdims=True)) + eps_norm)
            fresh = jnp.concatenate([k_hat.reshape(IMG, HW).astype(jnp.bfloat16), v.astype(jnp.bfloat16)], -1)
            query = (q_hat * score_gain[layer] / math.sqrt(HEAD)).astype(jnp.bfloat16)
            pieces = []
            for patch in range(N_PATCH):
                low = patch * IMG_DEV
                high = low + IMG_DEV
                mixed = jnp.concatenate([stale_r[layer, :low], fresh[low:high], stale_r[layer, high:]], 0)
                keys_all = jnp.concatenate([text_r[layer], mixed], 0)
                pieces.append(attend(query[low:high], keys_all))
            attn = jnp.concatenate(pieces, 0)
            proj = jnp.dot(attn, out_weight[layer], preferred_element_type=jnp.float32)
            x = (xf + mod_r[layer, 2] * proj).astype(jnp.bfloat16)
            fresh_list.append(fresh)
        final = modulated(x.astype(jnp.float32), fmod[0], fmod[1]).astype(jnp.bfloat16)
        velocity = jnp.dot(final, final_weight, preferred_element_type=jnp.float32)
        sig = sigma_of(step)
        sig_next = sigma_of(step + 1)
        return (jnp.stack(fresh_list), lat + (sig_next - sig) * velocity, lat - sig * velocity)
    fresh_all, latent_next, denoised = lax.map(one_request, (hidden, jnp.transpose(text_kv, (1, 0, 2, 3)), jnp.transpose(stale_kv, (1, 0, 2, 3)), jnp.transpose(modulation, (1, 0, 2, 3)), final_mod, latent, step_index))
    return (jnp.transpose(fresh_all, (1, 0, 2, 3)), latent_next, denoised)
```

```python
import functools
import math

import jax
import jax.numpy as jnp
from jax import lax
from jax.experimental import pallas as pl
from jax.experimental.pallas import tpu as pltpu
from jax.sharding import PartitionSpec as P

HEAD = 64
NSTEPS = 28
LANES = 128
BLOCK = 512

eps_norm = 1e-06
flow_shift = 3.0

PARAMS = pltpu.CompilerParams(vmem_limit_bytes=56 * 1024 * 1024)


def sigma_of(step):
    s = 1.0 - step.astype(jnp.float32) / NSTEPS
    return flow_shift * s / (1.0 + (flow_shift - 1.0) * s)


def modulated(xf, shift, scale):
    mean = jnp.mean(xf, -1, keepdims=True)
    cent = xf - mean
    var = jnp.mean(cent * cent, -1, keepdims=True)
    return cent * lax.rsqrt(var + eps_norm) * (1.0 + scale) + shift


def head_means(squares):
    row = lax.broadcasted_iota(jnp.int32, (LANES, LANES), 0) // HEAD
    col = lax.broadcasted_iota(jnp.int32, (LANES, LANES), 1) // HEAD
    same = jnp.where(row == col, 1.0 / HEAD, 0.0).astype(jnp.bfloat16)
    high = squares.astype(jnp.bfloat16)
    low = (squares - high.astype(jnp.float32)).astype(jnp.bfloat16)
    return jnp.dot(high, same, preferred_element_type=jnp.float32) + jnp.dot(
        low, same, preferred_element_type=jnp.float32
    )


def qkv_kernel(n_query, n_key, x_ref, mod_ref, gain_ref, w_ref, out_ref, normed_ref):
    step = pl.program_id(0)

    @pl.when(step == 0)
    def _():
        xf = x_ref[...].astype(jnp.float32)
        normed_ref[...] = modulated(xf, mod_ref[0:1, :], mod_ref[1:2, :]).astype(jnp.bfloat16)

    proj = jnp.dot(normed_ref[...], w_ref[...], preferred_element_type=jnp.float32)
    for low in range(0, BLOCK, LANES):
        part = proj[:, low : low + LANES]
        col = step * BLOCK + low + lax.broadcasted_iota(jnp.int32, (1, LANES), 1)
        factor = lax.rsqrt(head_means(part * part) + eps_norm)
        scaled = part * factor * jnp.where(col < n_query, gain_ref[...], 1.0)
        out_ref[:, low : low + LANES] = jnp.where(col < n_query + n_key, scaled, part).astype(
            jnp.bfloat16
        )


def qkv(x, mod_one, gain, w, n_query, n_key):
    rows, depth = x.shape
    columns = w.shape[1]
    gain_row = jnp.tile(gain / math.sqrt(HEAD), LANES // HEAD)[None]
    return pl.pallas_call(
        functools.partial(qkv_kernel, n_query, n_key),
        grid=(pl.cdiv(columns, BLOCK),),
        in_specs=[
            pl.BlockSpec((rows, depth), lambda i: (0, 0)),
            pl.BlockSpec((3, depth), lambda i: (0, 0)),
            pl.BlockSpec((1, LANES), lambda i: (0, 0)),
            pl.BlockSpec((depth, BLOCK), lambda i: (0, i)),
        ],
        out_specs=pl.BlockSpec((rows, BLOCK), lambda i: (0, i)),
        out_shape=jax.ShapeDtypeStruct((rows, columns), jnp.bfloat16),
        scratch_shapes=[pltpu.VMEM((rows, depth), jnp.bfloat16)],
        compiler_params=PARAMS,
        cost_estimate=pl.CostEstimate(
            flops=2 * rows * depth * columns,
            bytes_accessed=2 * (depth * columns + rows * depth + rows * columns),
            transcendentals=0,
        ),
    )(x, mod_one, gain_row, w)


def attend_kernel(n_sets, *refs):
    q_ref, out_ref = refs[0], refs[-1]
    sets = [refs[1 + 3 * s : 4 + 3 * s] for s in range(n_sets)]
    query = q_ref[...]
    lane = lax.broadcasted_iota(jnp.int32, (1, LANES), 1)
    halves = []
    for head in range(2):
        mine = (lane >= HEAD) == (head == 1)
        q_one = jnp.where(mine, query, jnp.zeros_like(query))
        total = None
        for keys, value_even, value_odd in sets:
            values = (value_even, value_odd)[head]
            scores = lax.dot_general(
                q_one, keys[...], (((1,), (1,)), ((), ())), preferred_element_type=jnp.float32
            )
            weights = jnp.exp(scores).astype(jnp.bfloat16)
            held = jnp.where(mine, jnp.ones((), jnp.bfloat16), values[...])
            part = jnp.dot(weights, held, preferred_element_type=jnp.float32)
            total = part if total is None else total + part
        halves.append(pltpu.roll(total, HEAD, 1) / total)
    out_ref[...] = jnp.where(lane < HEAD, halves[0], halves[1]).astype(jnp.bfloat16)


def attend(qkv_out, n_query, sets, width):
    rows = qkv_out.shape[0]
    pairs = n_query // LANES
    own = n_query // LANES
    last = 2 * width // LANES - 1
    first_value = width // LANES

    def specs(count, offset):
        return [
            pl.BlockSpec((count, LANES), lambda i: (0, offset + i)),
            pl.BlockSpec((count, LANES), lambda i: (0, offset + first_value + i)),
            pl.BlockSpec(
                (count, LANES), lambda i: (0, offset + jnp.minimum(first_value + 1 + i, last))
            ),
        ]

    in_specs = [pl.BlockSpec((rows, LANES), lambda i: (0, i))]
    operands = [qkv_out]
    for array, offset in [(qkv_out, own)] + [(array, 0) for array in sets]:
        in_specs += specs(array.shape[0], offset)
        operands += [array] * 3
    count = rows + sum(array.shape[0] for array in sets)
    return pl.pallas_call(
        functools.partial(attend_kernel, 1 + len(sets)),
        grid=(pairs,),
        in_specs=in_specs,
        out_specs=pl.BlockSpec((rows, LANES), lambda i: (0, i)),
        out_shape=jax.ShapeDtypeStruct((rows, n_query), jnp.bfloat16),
        compiler_params=PARAMS,
        cost_estimate=pl.CostEstimate(
            flops=16 * rows * count * width,
            bytes_accessed=4 * count * width,
            transcendentals=rows * count * width // HEAD,
        ),
    )(*operands)


def out_kernel(width, x_ref, attn_ref, mod_ref, w_ref, *rest):
    attn = attn_ref[:, :width]
    proj = jnp.concatenate(
        [
            jnp.dot(attn, w_ref[shard], preferred_element_type=jnp.float32)
            for shard in range(w_ref.shape[0])
        ],
        -1,
    )
    x_next = (x_ref[...].astype(jnp.float32) + mod_ref[2:3, :] * proj).astype(jnp.bfloat16)
    if len(rest) == 1:
        rest[0][...] = x_next
        return
    fmod_ref, fw_ref, vel_ref = rest
    final = modulated(x_next.astype(jnp.float32), fmod_ref[0:1, :], fmod_ref[1:2, :])
    vel_ref[...] = jnp.dot(
        final.astype(jnp.bfloat16), fw_ref[...], preferred_element_type=jnp.float32
    )


def project_out(x, attn, mod_one, w, final=None):
    rows, depth = x.shape
    width = w.shape[1]
    operands = [x, attn, mod_one, w]
    if final is None:
        shape = jax.ShapeDtypeStruct((rows, depth), jnp.bfloat16)
    else:
        operands += list(final)
        shape = jax.ShapeDtypeStruct((rows, final[1].shape[1]), jnp.float32)
    return pl.pallas_call(
        functools.partial(out_kernel, width),
        in_specs=[pl.BlockSpec(memory_space=pltpu.VMEM)] * len(operands),
        out_specs=pl.BlockSpec(memory_space=pltpu.VMEM),
        out_shape=shape,
        compiler_params=PARAMS,
        cost_estimate=pl.CostEstimate(
            flops=2 * rows * depth * width,
            bytes_accessed=2 * (depth * width + 3 * rows * depth),
            transcendentals=0,
        ),
    )(*operands)


def on_device(
    hidden,
    text_kv,
    stale_kv,
    modulation,
    score_gain,
    qkv_weight,
    out_weight,
    final_mod,
    final_weight,
    latent,
    step_index,
):
    section = lax.axis_index("section")
    patch = lax.axis_index("patch")
    patches = lax.axis_size("patch")
    shards = lax.axis_size("shard")
    requests, rows, depth = hidden.shape
    width = out_weight.shape[1]
    n_query = pl.cdiv(width, LANES) * LANES

    share = qkv_weight.shape[1] // patches
    mine = lax.dynamic_slice_in_dim(qkv_weight[0], patch * share, share, 0)
    mine = jnp.concatenate(
        [mine[:, :width], jnp.zeros((share, n_query - width), mine.dtype), mine[:, width:]], 1
    )
    w_qkv = lax.all_gather(mine, ("shard", "patch"), axis=0, tiled=True)
    stale = [stale_kv[0]]
    step = patches // 2
    while step >= 1:
        pairs = [(p, p ^ step) for p in range(patches)]
        stale = stale + [lax.ppermute(array, "patch", pairs) for array in stale]
        step //= 2
    stale = stale[1:]
    share = width // patches
    mine = lax.dynamic_slice_in_dim(out_weight[0], patch * share, share, 0)
    w_out = lax.all_gather(mine, ("shard", "patch"), axis=0, tiled=True)
    w_out = w_out.reshape(shards, width, out_weight.shape[2])

    def layer(r, x, final=None):
        mod_one = modulation[0, r]
        held = qkv(x, mod_one, score_gain[0], w_qkv, n_query, width)
        sets = [array[r] for array in stale] + [text_kv[0, r]]
        attn = attend(held, n_query, sets, width)
        return project_out(x, attn, mod_one, w_out, final), held[:, n_query:]

    hop = [(s, s + 1) for s in range(lax.axis_size("section") - 1)]
    arrived, fresh_first, fresh_last, velocity = [], [], [], []
    for r in range(requests):
        x_next, fresh = layer(r, hidden[r])
        arrived.append(lax.ppermute(x_next, "section", hop))
        fresh_first.append(fresh)
    for r in range(requests):
        vel, fresh = layer(r, arrived[r], (final_mod[r], final_weight))
        velocity.append(vel)
        fresh_last.append(fresh)
    fresh = jnp.where(section == 0, jnp.stack(fresh_first), jnp.stack(fresh_last))
    velocity = jnp.stack(velocity)
    half = latent.shape[1]
    back = lax.ppermute(velocity[:, :half].astype(jnp.bfloat16), "section", [(1, 0)])
    velocity_mine = jnp.where(section == 0, back.astype(jnp.float32), velocity[:, half:])
    sig = sigma_of(step_index)[:, None, None]
    sig_next = sigma_of(step_index + 1)[:, None, None]
    latent_next = latent + (sig_next - sig) * velocity_mine
    denoised = latent - sig * velocity_mine
    return (fresh[None], latent_next, denoised)


def solution(mesh):
    in_specs = (
        P("shard", "patch", None),
        P("section", "shard", None, None),
        P("section", "shard", "patch", None),
        P("section", "shard", None, None),
        P("section", None),
        P("section", "shard", None),
        P("section", None, "shard"),
        P("shard", None, None),
        P(),
        P("shard", ("patch", "section"), None),
        P("shard"),
    )
    out_specs = (
        P("section", "shard", "patch", None),
        P("shard", ("patch", "section"), None),
        P("shard", ("patch", "section"), None),
    )
    return jax.shard_map(
        on_device, mesh=mesh, in_specs=in_specs, out_specs=out_specs, check_vma=False
    )
```

```python
import functools
import math

import jax
import jax.numpy as jnp
from jax import lax
from jax.experimental import pallas as pl
from jax.experimental.pallas import tpu as pltpu
from jax.sharding import PartitionSpec as P

HEAD = 64
NSTEPS = 28
LANES = 128
BLOCK = 768

eps_norm = 1e-06
flow_shift = 3.0

PARAMS = pltpu.CompilerParams(vmem_limit_bytes=56 * 1024 * 1024)


def sigma_of(step):
    s = 1.0 - step.astype(jnp.float32) / NSTEPS
    return flow_shift * s / (1.0 + (flow_shift - 1.0) * s)


def modulated(xf, shift, scale):
    mean = jnp.mean(xf, -1, keepdims=True)
    cent = xf - mean
    var = jnp.mean(cent * cent, -1, keepdims=True)
    return cent * lax.rsqrt(var + eps_norm) * (1.0 + scale) + shift


def head_means(squares):
    row = lax.broadcasted_iota(jnp.int32, (LANES, LANES), 0) // HEAD
    col = lax.broadcasted_iota(jnp.int32, (LANES, LANES), 1) // HEAD
    same = jnp.where(row == col, 1.0 / HEAD, 0.0).astype(jnp.bfloat16)
    high = squares.astype(jnp.bfloat16)
    low = (squares - high.astype(jnp.float32)).astype(jnp.bfloat16)
    return jnp.dot(high, same, preferred_element_type=jnp.float32) + jnp.dot(
        low, same, preferred_element_type=jnp.float32
    )


def qkv_kernel(n_query, n_key, x_ref, mod_ref, gain_ref, w_ref, out_ref, normed_ref):
    step = pl.program_id(0)

    @pl.when(step == 0)
    def _():
        xf = x_ref[...].astype(jnp.float32)
        normed_ref[...] = modulated(xf, mod_ref[0:1, :], mod_ref[1:2, :]).astype(jnp.bfloat16)

    proj = jnp.dot(normed_ref[...], w_ref[...], preferred_element_type=jnp.float32)
    for low in range(0, BLOCK, LANES):
        part = proj[:, low : low + LANES]
        col = step * BLOCK + low + lax.broadcasted_iota(jnp.int32, (1, LANES), 1)
        factor = lax.rsqrt(head_means(part * part) + eps_norm)
        scaled = part * factor * jnp.where(col < n_query, gain_ref[...], 1.0)
        out_ref[:, low : low + LANES] = jnp.where(col < n_query + n_key, scaled, part).astype(
            jnp.bfloat16
        )


def picked(array, lead, shape, index):
    return pl.BlockSpec(
        (None,) * len(lead) + shape, lambda *grid: tuple(lead) + tuple(index(*grid))
    )


def qkv(x, x_lead, modulation, r, gain, w, n_query, n_key):
    rows, depth = x.shape[-2:]
    columns = w.shape[1]
    gain_row = jnp.tile(gain / math.sqrt(HEAD), LANES // HEAD)[None]
    return pl.pallas_call(
        functools.partial(qkv_kernel, n_query, n_key),
        grid=(pl.cdiv(columns, BLOCK),),
        in_specs=[
            picked(x, x_lead, (rows, depth), lambda i: (0, 0)),
            picked(modulation, (0, r), (3, depth), lambda i: (0, 0)),
            pl.BlockSpec((1, LANES), lambda i: (0, 0)),
            pl.BlockSpec((depth, BLOCK), lambda i: (0, i)),
        ],
        out_specs=pl.BlockSpec((rows, BLOCK), lambda i: (0, i)),
        out_shape=jax.ShapeDtypeStruct((rows, columns), jnp.bfloat16),
        scratch_shapes=[pltpu.VMEM((rows, depth), jnp.bfloat16)],
        compiler_params=PARAMS,
        cost_estimate=pl.CostEstimate(
            flops=2 * rows * depth * columns,
            bytes_accessed=2 * (depth * columns + rows * depth + rows * columns),
            transcendentals=0,
        ),
    )(x, modulation, gain_row, w)


def attend_kernel(n_sets, *refs):
    q_ref, out_ref = refs[0], refs[-1]
    sets = [refs[1 + 3 * s : 4 + 3 * s] for s in range(n_sets)]
    query = q_ref[...]
    lane = lax.broadcasted_iota(jnp.int32, (1, LANES), 1)
    halves = []
    for head in range(2):
        mine = (lane >= HEAD) == (head == 1)
        q_one = jnp.where(mine, query, jnp.zeros_like(query))
        total = None
        for keys, value_even, value_odd in sets:
            values = (value_even, value_odd)[head]
            scores = lax.dot_general(
                q_one, keys[...], (((1,), (1,)), ((), ())), preferred_element_type=jnp.float32
            )
            weights = jnp.exp(scores).astype(jnp.bfloat16)
            held = jnp.where(mine, jnp.ones((), jnp.bfloat16), values[...])
            part = jnp.dot(weights, held, preferred_element_type=jnp.float32)
            total = part if total is None else total + part
        halves.append(pltpu.roll(total, HEAD, 1) / total)
    out_ref[...] = jnp.where(lane < HEAD, halves[0], halves[1]).astype(jnp.bfloat16)


def attend(qkv_out, n_query, sets, width):
    rows = qkv_out.shape[0]
    pairs = n_query // LANES
    own = n_query // LANES
    last = 2 * width // LANES - 1
    first_value = width // LANES

    def specs(array, lead, offset):
        shape = (array.shape[-2], LANES)
        return [
            picked(array, lead, shape, lambda i: (0, offset + i)),
            picked(array, lead, shape, lambda i: (0, offset + first_value + i)),
            picked(
                array,
                lead,
                shape,
                lambda i: (0, offset + jnp.minimum(first_value + 1 + i, last)),
            ),
        ]

    in_specs = [pl.BlockSpec((rows, LANES), lambda i: (0, i))]
    operands = [qkv_out]
    for array, lead, offset in [(qkv_out, (), own)] + [pair + (0,) for pair in sets]:
        in_specs += specs(array, lead, offset)
        operands += [array] * 3
    count = rows + sum(array.shape[-2] for array, _ in sets)
    return pl.pallas_call(
        functools.partial(attend_kernel, 1 + len(sets)),
        grid=(pairs,),
        in_specs=in_specs,
        out_specs=pl.BlockSpec((rows, LANES), lambda i: (0, i)),
        out_shape=jax.ShapeDtypeStruct((rows, n_query), jnp.bfloat16),
        compiler_params=PARAMS,
        cost_estimate=pl.CostEstimate(
            flops=16 * rows * count * width,
            bytes_accessed=4 * count * width,
            transcendentals=rows * count * width // HEAD,
        ),
    )(*operands)


def out_kernel(width, x_ref, attn_ref, mod_ref, w_ref, *rest):
    attn = attn_ref[:, :width]
    proj = jnp.concatenate(
        [
            jnp.dot(attn, w_ref[shard], preferred_element_type=jnp.float32)
            for shard in range(w_ref.shape[0])
        ],
        -1,
    )
    x_next = (x_ref[...].astype(jnp.float32) + mod_ref[2:3, :] * proj).astype(jnp.bfloat16)
    if len(rest) == 1:
        rest[0][...] = x_next
        return
    fmod_ref, fw_ref, vel_ref = rest
    final = modulated(x_next.astype(jnp.float32), fmod_ref[0:1, :], fmod_ref[1:2, :])
    vel_ref[...] = jnp.dot(
        final.astype(jnp.bfloat16), fw_ref[...], preferred_element_type=jnp.float32
    )


def project_out(x, x_lead, attn, modulation, r, w, final=None):
    rows, depth = x.shape[-2:]
    width = w.shape[1]
    operands = [x, attn, modulation, w]
    specs = [
        picked(x, x_lead, (rows, depth), lambda i: (0, 0)),
        pl.BlockSpec(attn.shape, lambda i: (0, 0)),
        picked(modulation, (0, r), (3, depth), lambda i: (0, 0)),
        pl.BlockSpec(w.shape, lambda i: (0, 0, 0)),
    ]
    if final is None:
        shape = jax.ShapeDtypeStruct((rows, depth), jnp.bfloat16)
    else:
        operands += list(final)
        specs.append(picked(final[0], (r,), final[0].shape[1:], lambda i: (0, 0)))
        specs.append(pl.BlockSpec(final[1].shape, lambda i: (0, 0)))
        shape = jax.ShapeDtypeStruct((rows, final[1].shape[1]), jnp.float32)
    return pl.pallas_call(
        functools.partial(out_kernel, width),
        grid=(1,),
        in_specs=specs,
        out_specs=pl.BlockSpec(shape.shape, lambda i: (0, 0)),
        out_shape=shape,
        compiler_params=PARAMS,
        cost_estimate=pl.CostEstimate(
            flops=2 * rows * depth * width,
            bytes_accessed=2 * (depth * width + 3 * rows * depth),
            transcendentals=0,
        ),
    )(*operands)


MESH = pl.DeviceIdType.MESH
LAG = 3


def row_chunks(rows):
    first = pl.cdiv(rows // 16, 2) * 16
    return ((0, first), (first, rows - first))


def gather_kernel(
    n, w_ref, wo_ref, stale_ref, w_all, wo_all, stale_all, own, zs, zr, hs, hr, os_, or_, ss, sr
):
    me = lax.axis_index("shard")
    patch = lax.axis_index("patch")
    rows, columns = w_ref.shape
    half_rows, half_columns = rows // 2, columns // 2
    o_rows = wo_ref.shape[0] // 2
    chunks = row_chunks(half_rows)
    requests = stale_ref.shape[0]
    has_left, has_right = me > 0, me < n - 1

    barrier = pltpu.get_barrier_semaphore()
    for other in (1, 2):
        pl.semaphore_signal(
            barrier, inc=1, device_id={"patch": patch ^ other}, device_id_type=MESH
        )

    @pl.when(has_left)
    def _():
        pl.semaphore_signal(barrier, inc=1, device_id={"shard": me - 1}, device_id_type=MESH)

    @pl.when(has_right)
    def _():
        pl.semaphore_signal(barrier, inc=1, device_id={"shard": me + 1}, device_id_type=MESH)

    pl.semaphore_wait(
        barrier, 2 + jnp.where(has_left, 1, 0) + jnp.where(has_right, 1, 0)
    )

    def spot(ref, base, quarter, k):
        start, size = chunks[k]
        return ref.at[
            pl.ds(pl.multiple_of(base + (quarter // 2) * half_rows + start, 16), size),
            pl.ds(pl.multiple_of((quarter % 2) * half_columns, LANES), half_columns),
        ]

    def block(way, t):
        return me - t if way == 0 else me + t

    def incoming(way, t):
        return (me - 1 - t >= 0) if way == 0 else (me + 1 + t < n)

    def ahead(way):
        return has_right if way == 0 else has_left

    def z_copy(way, t, k, sending):
        b = block(way, t if sending else t + 1)
        dst = spot(w_all, b * rows, patch, k)
        src = spot(w_ref, 0, patch, k) if sending and t == 0 else dst
        return pltpu.make_async_remote_copy(
            src_ref=src,
            dst_ref=dst,
            send_sem=zs.at[way, t, k],
            recv_sem=zr.at[way, t, k],
            device_id={"shard": me + 1 if way == 0 else me - 1},
            device_id_type=MESH,
        )

    def hop(kind, way, t, k, sending):
        to = 2 if kind == 0 else 1
        held = patch ^ 2 if kind == 2 else patch
        place = spot(w_all, block(way, t + 1) * rows, held if sending else held ^ to, k)
        return pltpu.make_async_remote_copy(
            src_ref=place,
            dst_ref=place,
            send_sem=hs.at[kind, way, t, k],
            recv_sem=hr.at[kind, way, t, k],
            device_id={"patch": patch ^ to},
            device_id_type=MESH,
        )

    def o_copy(way, t, sending):
        b = block(way, t if sending else t + 1)
        half = pl.ds(pl.multiple_of((patch % 2) * o_rows, 16), o_rows)
        dst = wo_all.at[b, half]
        src = wo_ref.at[half] if sending and t == 0 else dst
        return pltpu.make_async_remote_copy(
            src_ref=src,
            dst_ref=dst,
            send_sem=os_.at[0, way, t],
            recv_sem=or_.at[0, way, t],
            device_id={"shard": me + 1 if way == 0 else me - 1},
            device_id_type=MESH,
        )

    def o_hop(way, t, sending):
        parity = patch % 2 if sending else 1 - patch % 2
        place = wo_all.at[
            block(way, t + 1), pl.ds(pl.multiple_of(parity * o_rows, 16), o_rows)
        ]
        return pltpu.make_async_remote_copy(
            src_ref=place,
            dst_ref=place,
            send_sem=os_.at[1, way, t],
            recv_sem=or_.at[1, way, t],
            device_id={"patch": patch ^ 1},
            device_id_type=MESH,
        )

    def s_copy(kind, r):
        return pltpu.make_async_remote_copy(
            src_ref=stale_all.at[0, r] if kind == 2 else stale_ref.at[r],
            dst_ref=stale_all.at[kind, r],
            send_sem=ss.at[kind, r],
            recv_sem=sr.at[kind, r],
            device_id={"patch": patch ^ (2 if kind == 0 else 1)},
            device_id_type=MESH,
        )

    for way in range(2):

        @pl.when(ahead(way))
        def _(way=way):
            for k in range(len(chunks)):
                z_copy(way, 0, k, True).start()

    s_copy(0, 0).start()
    for r in range(requests):
        s_copy(1, r).start()
    own_w = pltpu.make_async_copy(
        w_ref, w_all.at[pl.ds(pl.multiple_of(me * rows, 16), rows)], own.at[0]
    )
    own_o = pltpu.make_async_copy(wo_ref, wo_all.at[me], own.at[1])
    own_w.start()
    own_o.start()

    items = [
        (way, t, k) for t in range(n - 1) for k in range(len(chunks)) for way in range(2)
    ]

    def pass_on(way, t, k):
        @pl.when(incoming(way, t))
        def _():
            hop(0, way, t, k, False).wait_recv()
            hop(2, way, t, k, True).start()

    for place, (way, t, k) in enumerate(items):

        @pl.when(incoming(way, t))
        def _(way=way, t=t, k=k):
            z_copy(way, t, k, False).wait_recv()
            if t + 1 < n - 1:

                @pl.when(ahead(way))
                def _():
                    z_copy(way, t + 1, k, True).start()

            hop(0, way, t, k, True).start()
            hop(1, way, t, k, True).start()

        if place >= 2 * LAG:
            pass_on(*items[place - 2 * LAG])
        if t == max(n - 3, 0) and k == len(chunks) - 1:

            @pl.when(ahead(way))
            def _(way=way):
                o_copy(way, 0, True).start()

    for r in range(1, requests):
        s_copy(0, r).start()
    s_copy(0, 0).wait_recv()
    s_copy(2, 0).start()
    for place in range(max(len(items) - 2 * LAG, 0), len(items)):
        pass_on(*items[place])
    for t in range(n - 1):
        for way in range(2):

            @pl.when(incoming(way, t))
            def _(way=way, t=t):
                o_copy(way, t, False).wait_recv()
                if t + 1 < n - 1:

                    @pl.when(ahead(way))
                    def _():
                        o_copy(way, t + 1, True).start()

                o_hop(way, t, True).start()

    for r in range(1, requests):
        s_copy(0, r).wait_recv()
        s_copy(2, r).start()
    for way, t, k in items:

        @pl.when(incoming(way, t))
        def _(way=way, t=t, k=k):
            for kind in range(3):
                hop(kind, way, t, k, True).wait_send()
            for kind in (1, 2):
                hop(kind, way, t, k, False).wait_recv()

        sends = incoming(way, t - 1) if t > 0 else True

        @pl.when(jnp.logical_and(ahead(way), sends))
        def _(way=way, t=t, k=k):
            z_copy(way, t, k, True).wait_send()

        if k == 0:

            @pl.when(incoming(way, t))
            def _(way=way, t=t):
                o_hop(way, t, True).wait_send()
                o_hop(way, t, False).wait_recv()

            @pl.when(jnp.logical_and(ahead(way), sends))
            def _(way=way, t=t):
                o_copy(way, t, True).wait_send()

    for r in range(requests):
        for kind in range(3):
            s_copy(kind, r).wait_send()
        for kind in (1, 2):
            s_copy(kind, r).wait_recv()
    own_w.wait()
    own_o.wait()


def gather(w, w_out, stale, n):
    rows, columns = w.shape
    anywhere = pl.BlockSpec(memory_space=pl.ANY)
    dma = pltpu.SemaphoreType.DMA
    requests = stale.shape[0]
    return pl.pallas_call(
        functools.partial(gather_kernel, n),
        in_specs=[anywhere] * 3,
        out_specs=[anywhere] * 3,
        out_shape=[
            jax.ShapeDtypeStruct((n * rows, columns), w.dtype),
            jax.ShapeDtypeStruct((n,) + w_out.shape, w_out.dtype),
            jax.ShapeDtypeStruct((3,) + stale.shape, stale.dtype),
        ],
        scratch_shapes=[
            dma((2,)),
            dma((2, n - 1, 2)),
            dma((2, n - 1, 2)),
            dma((3, 2, n - 1, 2)),
            dma((3, 2, n - 1, 2)),
            dma((2, 2, n - 1)),
            dma((2, 2, n - 1)),
            dma((3, requests)),
            dma((3, requests)),
        ],
        compiler_params=pltpu.CompilerParams(
            collective_id=0, has_side_effects=True, vmem_limit_bytes=56 * 1024 * 1024
        ),
        cost_estimate=pl.CostEstimate(
            flops=0, bytes_accessed=4 * n * rows * columns, transcendentals=0
        ),
    )(w, w_out, stale)


def on_device(
    hidden,
    text_kv,
    stale_kv,
    modulation,
    score_gain,
    qkv_weight,
    out_weight,
    final_mod,
    final_weight,
    latent,
    step_index,
):
    section = lax.axis_index("section")
    patch = lax.axis_index("patch")
    patches = lax.axis_size("patch")
    shards = lax.axis_size("shard")
    requests, rows, depth = hidden.shape
    width = out_weight.shape[1]
    n_query = pl.cdiv(width, LANES) * LANES

    columns = pl.cdiv(n_query + 2 * width, 2 * LANES) * 2 * LANES
    w = qkv_weight[0]
    packed = jnp.concatenate(
        [
            w[:, :width],
            jnp.zeros((w.shape[0], n_query - width), w.dtype),
            w[:, width:],
            jnp.zeros((w.shape[0], columns - n_query - 2 * width), w.dtype),
        ],
        1,
    )
    if patches == 4 and w.shape[0] % 32 == 0 and width % 32 == 0:
        w_qkv, w_out, stale = gather(packed, out_weight[0], stale_kv[0], shards)
        stale = [(stale, (i,)) for i in range(3)]
    else:
        share = w.shape[0] // patches
        mine = lax.dynamic_slice_in_dim(packed, patch * share, share, 0)
        w_qkv = lax.all_gather(mine, ("shard", "patch"), axis=0, tiled=True)
        share = width // patches
        mine = lax.dynamic_slice_in_dim(out_weight[0], patch * share, share, 0)
        w_out = lax.all_gather(mine, ("shard", "patch"), axis=0, tiled=True)
        w_out = w_out.reshape(shards, width, out_weight.shape[2])
        stale = [stale_kv[0]]
        step = patches // 2
        while step >= 1:
            pairs = [(p, p ^ step) for p in range(patches)]
            stale = stale + [lax.ppermute(array, "patch", pairs) for array in stale]
            step //= 2
        stale = [(array, ()) for array in stale[1:]]

    def layer(r, x, x_lead, final=None):
        held = qkv(x, x_lead, modulation, r, score_gain[0], w_qkv, n_query, width)
        sets = [(array, lead + (r,)) for array, lead in stale] + [(text_kv, (0, r))]
        attn = attend(held, n_query, sets, width)
        fresh = held[:, n_query : n_query + 2 * width]
        return project_out(x, x_lead, attn, modulation, r, w_out, final), fresh

    hop = [(s, s + 1) for s in range(lax.axis_size("section") - 1)]
    arrived, fresh_first, fresh_last, velocity = [], [], [], []
    for r in range(requests):
        x_next, fresh = layer(r, hidden, (r,))
        arrived.append(lax.ppermute(x_next, "section", hop))
        fresh_first.append(fresh)
    for r in range(requests):
        vel, fresh = layer(r, arrived[r], (), (final_mod, final_weight))
        velocity.append(vel)
        fresh_last.append(fresh)
    fresh = jnp.where(section == 0, jnp.stack(fresh_first), jnp.stack(fresh_last))
    velocity = jnp.stack(velocity)
    half = latent.shape[1]
    back = lax.ppermute(velocity[:, :half].astype(jnp.bfloat16), "section", [(1, 0)])
    velocity_mine = jnp.where(section == 0, back.astype(jnp.float32), velocity[:, half:])
    sig = sigma_of(step_index)[:, None, None]
    sig_next = sigma_of(step_index + 1)[:, None, None]
    latent_next = latent + (sig_next - sig) * velocity_mine
    denoised = latent - sig * velocity_mine
    return (fresh[None], latent_next, denoised)


def solution(mesh):
    in_specs = (
        P("shard", "patch", None),
        P("section", "shard", None, None),
        P("section", "shard", "patch", None),
        P("section", "shard", None, None),
        P("section", None),
        P("section", "shard", None),
        P("section", None, "shard"),
        P("shard", None, None),
        P(),
        P("shard", ("patch", "section"), None),
        P("shard"),
    )
    out_specs = (
        P("section", "shard", "patch", None),
        P("shard", ("patch", "section"), None),
        P("shard", ("patch", "section"), None),
    )
    return jax.shard_map(
        on_device, mesh=mesh, in_specs=in_specs, out_specs=out_specs, check_vma=False
    )
```

```python
import functools
import math

import jax
import jax.numpy as jnp
from jax import lax
from jax.experimental import pallas as pl
from jax.experimental.pallas import tpu as pltpu
from jax.sharding import PartitionSpec as P

HEAD = 64
NSTEPS = 28
LANES = 128
BLOCK = 768
PART = 256

eps_norm = 1e-06
flow_shift = 3.0

PARAMS = pltpu.CompilerParams(vmem_limit_bytes=56 * 1024 * 1024)


def sigma_of(step):
    s = 1.0 - step.astype(jnp.float32) / NSTEPS
    return flow_shift * s / (1.0 + (flow_shift - 1.0) * s)


def modulated(xf, shift, scale):
    mean = jnp.mean(xf, -1, keepdims=True)
    cent = xf - mean
    var = jnp.mean(cent * cent, -1, keepdims=True)
    return cent * lax.rsqrt(var + eps_norm) * (1.0 + scale) + shift


def head_means(squares):
    count = squares.shape[1]
    row = lax.broadcasted_iota(jnp.int32, (count, count), 0) // HEAD
    col = lax.broadcasted_iota(jnp.int32, (count, count), 1) // HEAD
    same = jnp.where(row == col, 1.0 / HEAD, 0.0).astype(jnp.bfloat16)
    high = squares.astype(jnp.bfloat16)
    low = (squares - high.astype(jnp.float32)).astype(jnp.bfloat16)
    return jnp.dot(high, same, preferred_element_type=jnp.float32) + jnp.dot(
        low, same, preferred_element_type=jnp.float32
    )


def qkv_kernel(n_query, n_key, x_ref, mod_ref, gain_ref, w_ref, out_ref, normed_ref):
    step = pl.program_id(0)

    @pl.when(step == 0)
    def _():
        xf = x_ref[...].astype(jnp.float32)
        normed_ref[...] = modulated(xf, mod_ref[0:1, :], mod_ref[1:2, :]).astype(jnp.bfloat16)

    for low in range(0, BLOCK, PART):
        part = jnp.dot(
            normed_ref[...], w_ref[:, low : low + PART], preferred_element_type=jnp.float32
        )
        first = step * BLOCK + low
        col = first + lax.broadcasted_iota(jnp.int32, (1, PART), 1)
        factor = lax.rsqrt(head_means(part * part) + eps_norm)
        factor = factor * jnp.where(col < n_query, gain_ref[...], 1.0)
        out_ref[:, low : low + PART] = (
            part * jnp.where(col < n_query + n_key, factor, 1.0)
        ).astype(jnp.bfloat16)


def picked(array, lead, shape, index):
    return pl.BlockSpec(
        (None,) * len(lead) + shape, lambda *grid: tuple(lead) + tuple(index(*grid))
    )


def qkv(x, x_lead, modulation, r, gain, w, n_query, n_key):
    rows, depth = x.shape[-2:]
    columns = w.shape[1]
    gain_row = jnp.tile(gain / math.sqrt(HEAD), PART // HEAD)[None]
    return pl.pallas_call(
        functools.partial(qkv_kernel, n_query, n_key),
        grid=(pl.cdiv(columns, BLOCK),),
        in_specs=[
            picked(x, x_lead, (rows, depth), lambda i: (0, 0)),
            picked(modulation, (0, r), (3, depth), lambda i: (0, 0)),
            pl.BlockSpec((1, PART), lambda i: (0, 0)),
            pl.BlockSpec((depth, BLOCK), lambda i: (0, i)),
        ],
        out_specs=pl.BlockSpec((rows, BLOCK), lambda i: (0, i)),
        out_shape=jax.ShapeDtypeStruct((rows, columns), jnp.bfloat16),
        scratch_shapes=[pltpu.VMEM((rows, depth), jnp.bfloat16)],
        compiler_params=PARAMS,
        cost_estimate=pl.CostEstimate(
            flops=2 * rows * depth * columns,
            bytes_accessed=2 * (depth * columns + rows * depth + rows * columns),
            transcendentals=0,
        ),
    )(x, modulation, gain_row, w)


def attend_kernel(n_sets, *refs):
    q_ref, out_ref = refs[0], refs[-1]
    sets = [refs[1 + 3 * s : 4 + 3 * s] for s in range(n_sets)]
    query = q_ref[...]
    rows = query.shape[0]
    lane = lax.broadcasted_iota(jnp.int32, (1, LANES), 1)
    low = lane < HEAD
    none = jnp.zeros((), jnp.bfloat16)
    one = jnp.ones((), jnp.bfloat16)
    both = jnp.concatenate([jnp.where(low, query, none), jnp.where(low, none, query)], 0)
    total = None
    for keys, value_even, value_odd in sets:
        scores = lax.dot_general(
            both, keys[...], (((1,), (1,)), ((), ())), preferred_element_type=jnp.float32
        )
        weights = jnp.exp(scores).astype(jnp.bfloat16)
        held = jnp.concatenate(
            [jnp.where(low, one, value_even[...]), jnp.where(low, value_odd[...], one)], 1
        )
        part = jnp.dot(weights, held, preferred_element_type=jnp.float32)
        total = part if total is None else total + part
    even, odd = total[:rows, :LANES], total[rows:, LANES:]
    halves = [pltpu.roll(each, HEAD, 1) / each for each in (even, odd)]
    out_ref[...] = jnp.where(lane < HEAD, halves[0], halves[1]).astype(jnp.bfloat16)


def attend(qkv_out, n_query, sets, width):
    rows = qkv_out.shape[0]
    pairs = n_query // LANES
    own = n_query // LANES
    last = 2 * width // LANES - 1
    first_value = width // LANES

    def specs(array, lead, offset):
        shape = (array.shape[-2], LANES)
        return [
            picked(array, lead, shape, lambda i: (0, offset + i)),
            picked(array, lead, shape, lambda i: (0, offset + first_value + i)),
            picked(
                array,
                lead,
                shape,
                lambda i: (0, offset + jnp.minimum(first_value + 1 + i, last)),
            ),
        ]

    in_specs = [pl.BlockSpec((rows, LANES), lambda i: (0, i))]
    operands = [qkv_out]
    for array, lead, offset in [(qkv_out, (), own)] + [pair + (0,) for pair in sets]:
        in_specs += specs(array, lead, offset)
        operands += [array] * 3
    count = rows + sum(array.shape[-2] for array, _ in sets)
    return pl.pallas_call(
        functools.partial(attend_kernel, 1 + len(sets)),
        grid=(pairs,),
        in_specs=in_specs,
        out_specs=pl.BlockSpec((rows, LANES), lambda i: (0, i)),
        out_shape=jax.ShapeDtypeStruct((rows, n_query), jnp.bfloat16),
        compiler_params=PARAMS,
        cost_estimate=pl.CostEstimate(
            flops=16 * rows * count * width,
            bytes_accessed=4 * count * width,
            transcendentals=rows * count * width // HEAD,
        ),
    )(*operands)


def out_kernel(width, x_ref, attn_ref, mod_ref, w_ref, *rest):
    step = pl.program_id(0)
    proj_ref = rest[-1]
    proj_ref[step] = jnp.dot(
        attn_ref[:, :width], w_ref[...], preferred_element_type=jnp.float32
    )

    @pl.when(step == pl.num_programs(0) - 1)
    def _():
        proj = jnp.concatenate([proj_ref[shard] for shard in range(proj_ref.shape[0])], -1)
        x_next = (x_ref[...].astype(jnp.float32) + mod_ref[2:3, :] * proj).astype(jnp.bfloat16)
        if len(rest) == 2:
            rest[0][...] = x_next
        else:
            fmod_ref, fw_ref, vel_ref = rest[:-1]
            final = modulated(x_next.astype(jnp.float32), fmod_ref[0:1, :], fmod_ref[1:2, :])
            vel_ref[...] = jnp.dot(
                final.astype(jnp.bfloat16), fw_ref[...], preferred_element_type=jnp.float32
            )


def project_out(x, x_lead, attn, modulation, r, w, final=None):
    rows, depth = x.shape[-2:]
    width = w.shape[1]
    operands = [x, attn, modulation, w]
    specs = [
        picked(x, x_lead, (rows, depth), lambda i: (0, 0)),
        pl.BlockSpec(attn.shape, lambda i: (0, 0)),
        picked(modulation, (0, r), (3, depth), lambda i: (0, 0)),
        pl.BlockSpec((None,) + w.shape[1:], lambda i: (i, 0, 0)),
    ]
    if final is None:
        shape = jax.ShapeDtypeStruct((rows, depth), jnp.bfloat16)
    else:
        operands += list(final)
        specs.append(picked(final[0], (r,), final[0].shape[1:], lambda i: (0, 0)))
        specs.append(pl.BlockSpec(final[1].shape, lambda i: (0, 0)))
        shape = jax.ShapeDtypeStruct((rows, final[1].shape[1]), jnp.float32)
    return pl.pallas_call(
        functools.partial(out_kernel, width),
        grid=(w.shape[0],),
        in_specs=specs,
        out_specs=pl.BlockSpec(shape.shape, lambda i: (0, 0)),
        out_shape=shape,
        scratch_shapes=[pltpu.VMEM((w.shape[0], rows, w.shape[2]), jnp.float32)],
        compiler_params=PARAMS,
        cost_estimate=pl.CostEstimate(
            flops=2 * rows * depth * width,
            bytes_accessed=2 * (depth * width + 3 * rows * depth),
            transcendentals=0,
        ),
    )(*operands)


MESH = pl.DeviceIdType.MESH
LAG = 3


def row_chunks(rows):
    first = pl.cdiv(rows // 16, 2) * 16
    return ((0, first), (first, rows - first))


def gather_kernel(
    n, w_ref, wo_ref, stale_ref, w_all, wo_all, stale_all, own, zs, zr, hs, hr, os_, or_, ss, sr
):
    me = lax.axis_index("shard")
    patch = lax.axis_index("patch")
    rows, columns = w_ref.shape
    half_rows, half_columns = rows // 2, columns // 2
    o_rows = wo_ref.shape[0] // 2
    chunks = row_chunks(half_rows)
    requests = stale_ref.shape[0]
    has_left, has_right = me > 0, me < n - 1

    barrier = pltpu.get_barrier_semaphore()
    for other in (1, 2):
        pl.semaphore_signal(
            barrier, inc=1, device_id={"patch": patch ^ other}, device_id_type=MESH
        )

    @pl.when(has_left)
    def _():
        pl.semaphore_signal(barrier, inc=1, device_id={"shard": me - 1}, device_id_type=MESH)

    @pl.when(has_right)
    def _():
        pl.semaphore_signal(barrier, inc=1, device_id={"shard": me + 1}, device_id_type=MESH)

    pl.semaphore_wait(
        barrier, 2 + jnp.where(has_left, 1, 0) + jnp.where(has_right, 1, 0)
    )

    def spot(ref, base, quarter, k):
        start, size = chunks[k]
        return ref.at[
            pl.ds(pl.multiple_of(base + (quarter // 2) * half_rows + start, 16), size),
            pl.ds(pl.multiple_of((quarter % 2) * half_columns, LANES), half_columns),
        ]

    def block(way, t):
        return me - t if way == 0 else me + t

    def incoming(way, t):
        return (me - 1 - t >= 0) if way == 0 else (me + 1 + t < n)

    def ahead(way):
        return has_right if way == 0 else has_left

    def z_copy(way, t, k, sending):
        b = block(way, t if sending else t + 1)
        dst = spot(w_all, b * rows, patch, k)
        src = spot(w_ref, 0, patch, k) if sending and t == 0 else dst
        return pltpu.make_async_remote_copy(
            src_ref=src,
            dst_ref=dst,
            send_sem=zs.at[way, t, k],
            recv_sem=zr.at[way, t, k],
            device_id={"shard": me + 1 if way == 0 else me - 1},
            device_id_type=MESH,
        )

    def hop(kind, way, t, k, sending):
        to = 2 if kind == 0 else 1
        held = patch ^ 2 if kind == 2 else patch
        place = spot(w_all, block(way, t + 1) * rows, held if sending else held ^ to, k)
        return pltpu.make_async_remote_copy(
            src_ref=place,
            dst_ref=place,
            send_sem=hs.at[kind, way, t, k],
            recv_sem=hr.at[kind, way, t, k],
            device_id={"patch": patch ^ to},
            device_id_type=MESH,
        )

    def o_copy(way, t, sending):
        b = block(way, t if sending else t + 1)
        half = pl.ds(pl.multiple_of((patch % 2) * o_rows, 16), o_rows)
        dst = wo_all.at[b, half]
        src = wo_ref.at[half] if sending and t == 0 else dst
        return pltpu.make_async_remote_copy(
            src_ref=src,
            dst_ref=dst,
            send_sem=os_.at[0, way, t],
            recv_sem=or_.at[0, way, t],
            device_id={"shard": me + 1 if way == 0 else me - 1},
            device_id_type=MESH,
        )

    def o_hop(way, t, sending):
        parity = patch % 2 if sending else 1 - patch % 2
        place = wo_all.at[
            block(way, t + 1), pl.ds(pl.multiple_of(parity * o_rows, 16), o_rows)
        ]
        return pltpu.make_async_remote_copy(
            src_ref=place,
            dst_ref=place,
            send_sem=os_.at[1, way, t],
            recv_sem=or_.at[1, way, t],
            device_id={"patch": patch ^ 1},
            device_id_type=MESH,
        )

    def s_copy(kind, r):
        return pltpu.make_async_remote_copy(
            src_ref=stale_all.at[0, r] if kind == 2 else stale_ref.at[r],
            dst_ref=stale_all.at[kind, r],
            send_sem=ss.at[kind, r],
            recv_sem=sr.at[kind, r],
            device_id={"patch": patch ^ (2 if kind == 0 else 1)},
            device_id_type=MESH,
        )

    for way in range(2):

        @pl.when(ahead(way))
        def _(way=way):
            for k in range(len(chunks)):
                z_copy(way, 0, k, True).start()

    s_copy(0, 0).start()
    for r in range(requests):
        s_copy(1, r).start()
    own_w = pltpu.make_async_copy(
        w_ref, w_all.at[pl.ds(pl.multiple_of(me * rows, 16), rows)], own.at[0]
    )
    own_o = pltpu.make_async_copy(wo_ref, wo_all.at[me], own.at[1])
    own_w.start()
    own_o.start()

    items = [
        (way, t, k) for t in range(n - 1) for k in range(len(chunks)) for way in range(2)
    ]

    def pass_on(way, t, k):
        @pl.when(incoming(way, t))
        def _():
            hop(0, way, t, k, False).wait_recv()
            hop(2, way, t, k, True).start()

    for place, (way, t, k) in enumerate(items):

        @pl.when(incoming(way, t))
        def _(way=way, t=t, k=k):
            z_copy(way, t, k, False).wait_recv()
            if t + 1 < n - 1:

                @pl.when(ahead(way))
                def _():
                    z_copy(way, t + 1, k, True).start()

            hop(0, way, t, k, True).start()
            hop(1, way, t, k, True).start()

        if place >= 2 * LAG:
            pass_on(*items[place - 2 * LAG])
        if t == max(n - 3, 0) and k == len(chunks) - 1:

            @pl.when(ahead(way))
            def _(way=way):
                o_copy(way, 0, True).start()

    for r in range(1, requests):
        s_copy(0, r).start()
    s_copy(0, 0).wait_recv()
    s_copy(2, 0).start()
    for place in range(max(len(items) - 2 * LAG, 0), len(items)):
        pass_on(*items[place])
    for t in range(n - 1):
        for way in range(2):

            @pl.when(incoming(way, t))
            def _(way=way, t=t):
                o_copy(way, t, False).wait_recv()
                if t + 1 < n - 1:

                    @pl.when(ahead(way))
                    def _():
                        o_copy(way, t + 1, True).start()

                o_hop(way, t, True).start()

    for r in range(1, requests):
        s_copy(0, r).wait_recv()
        s_copy(2, r).start()
    for way, t, k in items:

        @pl.when(incoming(way, t))
        def _(way=way, t=t, k=k):
            for kind in range(3):
                hop(kind, way, t, k, True).wait_send()
            for kind in (1, 2):
                hop(kind, way, t, k, False).wait_recv()

        sends = incoming(way, t - 1) if t > 0 else True

        @pl.when(jnp.logical_and(ahead(way), sends))
        def _(way=way, t=t, k=k):
            z_copy(way, t, k, True).wait_send()

        if k == 0:

            @pl.when(incoming(way, t))
            def _(way=way, t=t):
                o_hop(way, t, True).wait_send()
                o_hop(way, t, False).wait_recv()

            @pl.when(jnp.logical_and(ahead(way), sends))
            def _(way=way, t=t):
                o_copy(way, t, True).wait_send()

    for r in range(requests):
        for kind in range(3):
            s_copy(kind, r).wait_send()
        for kind in (1, 2):
            s_copy(kind, r).wait_recv()
    own_w.wait()
    own_o.wait()


def gather(w, w_out, stale, n):
    rows, columns = w.shape
    anywhere = pl.BlockSpec(memory_space=pl.ANY)
    dma = pltpu.SemaphoreType.DMA
    requests = stale.shape[0]
    return pl.pallas_call(
        functools.partial(gather_kernel, n),
        in_specs=[anywhere] * 3,
        out_specs=[anywhere] * 3,
        out_shape=[
            jax.ShapeDtypeStruct((n * rows, columns), w.dtype),
            jax.ShapeDtypeStruct((n,) + w_out.shape, w_out.dtype),
            jax.ShapeDtypeStruct((3,) + stale.shape, stale.dtype),
        ],
        scratch_shapes=[
            dma((2,)),
            dma((2, n - 1, 2)),
            dma((2, n - 1, 2)),
            dma((3, 2, n - 1, 2)),
            dma((3, 2, n - 1, 2)),
            dma((2, 2, n - 1)),
            dma((2, 2, n - 1)),
            dma((3, requests)),
            dma((3, requests)),
        ],
        compiler_params=pltpu.CompilerParams(
            collective_id=0, has_side_effects=True, vmem_limit_bytes=56 * 1024 * 1024
        ),
        cost_estimate=pl.CostEstimate(
            flops=0, bytes_accessed=4 * n * rows * columns, transcendentals=0
        ),
    )(w, w_out, stale)


def on_device(
    hidden,
    text_kv,
    stale_kv,
    modulation,
    score_gain,
    qkv_weight,
    out_weight,
    final_mod,
    final_weight,
    latent,
    step_index,
):
    section = lax.axis_index("section")
    patch = lax.axis_index("patch")
    patches = lax.axis_size("patch")
    shards = lax.axis_size("shard")
    requests, rows, depth = hidden.shape
    width = out_weight.shape[1]
    n_query = pl.cdiv(width, LANES) * LANES

    columns = pl.cdiv(n_query + 2 * width, 2 * LANES) * 2 * LANES
    w = qkv_weight[0]
    packed = jnp.concatenate(
        [
            w[:, :width],
            jnp.zeros((w.shape[0], n_query - width), w.dtype),
            w[:, width:],
            jnp.zeros((w.shape[0], columns - n_query - 2 * width), w.dtype),
        ],
        1,
    )
    if patches == 4 and w.shape[0] % 32 == 0 and width % 32 == 0:
        w_qkv, w_out, stale = gather(packed, out_weight[0], stale_kv[0], shards)
        stale = [(stale, (i,)) for i in range(3)]
    else:
        share = w.shape[0] // patches
        mine = lax.dynamic_slice_in_dim(packed, patch * share, share, 0)
        w_qkv = lax.all_gather(mine, ("shard", "patch"), axis=0, tiled=True)
        share = width // patches
        mine = lax.dynamic_slice_in_dim(out_weight[0], patch * share, share, 0)
        w_out = lax.all_gather(mine, ("shard", "patch"), axis=0, tiled=True)
        w_out = w_out.reshape(shards, width, out_weight.shape[2])
        stale = [stale_kv[0]]
        step = patches // 2
        while step >= 1:
            pairs = [(p, p ^ step) for p in range(patches)]
            stale = stale + [lax.ppermute(array, "patch", pairs) for array in stale]
            step //= 2
        stale = [(array, ()) for array in stale[1:]]

    def layer(r, x, x_lead, final=None):
        held = qkv(x, x_lead, modulation, r, score_gain[0], w_qkv, n_query, width)
        sets = [(array, lead + (r,)) for array, lead in stale] + [(text_kv, (0, r))]
        attn = attend(held, n_query, sets, width)
        fresh = held[:, n_query : n_query + 2 * width]
        return project_out(x, x_lead, attn, modulation, r, w_out, final), fresh

    hop = [(s, s + 1) for s in range(lax.axis_size("section") - 1)]
    arrived, fresh_first, fresh_last, velocity = [], [], [], []
    for r in range(requests):
        x_next, fresh = layer(r, hidden, (r,))
        arrived.append(lax.ppermute(x_next, "section", hop))
        fresh_first.append(fresh)
    for r in range(requests):
        vel, fresh = layer(r, arrived[r], (), (final_mod, final_weight))
        velocity.append(vel)
        fresh_last.append(fresh)
    fresh = jnp.where(section == 0, jnp.stack(fresh_first), jnp.stack(fresh_last))
    velocity = jnp.stack(velocity)
    half = latent.shape[1]
    back = lax.ppermute(velocity[:, :half].astype(jnp.bfloat16), "section", [(1, 0)])
    velocity_mine = jnp.where(section == 0, back.astype(jnp.float32), velocity[:, half:])
    sig = sigma_of(step_index)[:, None, None]
    sig_next = sigma_of(step_index + 1)[:, None, None]
    latent_next = latent + (sig_next - sig) * velocity_mine
    denoised = latent - sig * velocity_mine
    return (fresh[None], latent_next, denoised)


def solution(mesh):
    in_specs = (
        P("shard", "patch", None),
        P("section", "shard", None, None),
        P("section", "shard", "patch", None),
        P("section", "shard", None, None),
        P("section", None),
        P("section", "shard", None),
        P("section", None, "shard"),
        P("shard", None, None),
        P(),
        P("shard", ("patch", "section"), None),
        P("shard"),
    )
    out_specs = (
        P("section", "shard", "patch", None),
        P("shard", ("patch", "section"), None),
        P("shard", ("patch", "section"), None),
    )
    return jax.shard_map(
        on_device, mesh=mesh, in_specs=in_specs, out_specs=out_specs, check_vma=False
    )
```

```python
import functools
import math

import jax
import jax.numpy as jnp
from jax import lax
from jax.experimental import pallas as pl
from jax.experimental.pallas import tpu as pltpu
from jax.sharding import PartitionSpec as P

HEAD = 64
NSTEPS = 28
LANES = 128
BLOCK = 768

eps_norm = 1e-06
flow_shift = 3.0

PARAMS = pltpu.CompilerParams(vmem_limit_bytes=56 * 1024 * 1024)


def sigma_of(step):
    s = 1.0 - step.astype(jnp.float32) / NSTEPS
    return flow_shift * s / (1.0 + (flow_shift - 1.0) * s)


def modulated(xf, shift, scale):
    mean = jnp.mean(xf, -1, keepdims=True)
    cent = xf - mean
    var = jnp.mean(cent * cent, -1, keepdims=True)
    return cent * lax.rsqrt(var + eps_norm) * (1.0 + scale) + shift


def head_means(squares):
    row = lax.broadcasted_iota(jnp.int32, (LANES, LANES), 0) // HEAD
    col = lax.broadcasted_iota(jnp.int32, (LANES, LANES), 1) // HEAD
    same = jnp.where(row == col, 1.0 / HEAD, 0.0).astype(jnp.bfloat16)
    high = squares.astype(jnp.bfloat16)
    low = (squares - high.astype(jnp.float32)).astype(jnp.bfloat16)
    return jnp.dot(high, same, preferred_element_type=jnp.float32) + jnp.dot(
        low, same, preferred_element_type=jnp.float32
    )


def qkv_kernel(n_query, n_key, x_ref, mod_ref, gain_ref, w_ref, out_ref, normed_ref):
    qkv_step(pl.program_id(0), n_query, n_key, x_ref, mod_ref, gain_ref, w_ref, out_ref, normed_ref)


def qkv_step(step, n_query, n_key, x_ref, mod_ref, gain_ref, w_ref, out_ref, normed_ref):
    @pl.when(step == 0)
    def _():
        xf = x_ref[...].astype(jnp.float32)
        normed_ref[...] = modulated(xf, mod_ref[0:1, :], mod_ref[1:2, :]).astype(jnp.bfloat16)

    proj = jnp.dot(normed_ref[...], w_ref[...], preferred_element_type=jnp.float32)
    for low in range(0, BLOCK, LANES):
        part = proj[:, low : low + LANES]
        col = step * BLOCK + low + lax.broadcasted_iota(jnp.int32, (1, LANES), 1)
        factor = lax.rsqrt(head_means(part * part) + eps_norm)
        scaled = part * factor * jnp.where(col < n_query, gain_ref[...], 1.0)
        out_ref[:, low : low + LANES] = jnp.where(col < n_query + n_key, scaled, part).astype(
            jnp.bfloat16
        )


def pack_kernel(width, n_query, w_ref, out_ref):
    out_ref[...] = jnp.zeros_like(out_ref)
    out_ref[:, :width] = w_ref[:, :width]
    out_ref[:, n_query : n_query + 2 * width] = w_ref[:, width:]


def pack(w, width, n_query, columns):
    rows = w.shape[0]
    block = min(rows, 160)
    return pl.pallas_call(
        functools.partial(pack_kernel, width, n_query),
        grid=(pl.cdiv(rows, block),),
        in_specs=[pl.BlockSpec((block, w.shape[1]), lambda i: (i, 0))],
        out_specs=pl.BlockSpec((block, columns), lambda i: (i, 0)),
        out_shape=jax.ShapeDtypeStruct((rows, columns), w.dtype),
        compiler_params=PARAMS,
    )(w)


def picked(array, lead, shape, index):
    return pl.BlockSpec(
        (None,) * len(lead) + shape, lambda *grid: tuple(lead) + tuple(index(*grid))
    )


def qkv(x, x_lead, modulation, r, gain, w, n_query, n_key):
    rows, depth = x.shape[-2:]
    columns = w.shape[1]
    gain_row = jnp.tile(gain / math.sqrt(HEAD), LANES // HEAD)[None]
    return pl.pallas_call(
        functools.partial(qkv_kernel, n_query, n_key),
        grid=(pl.cdiv(columns, BLOCK),),
        in_specs=[
            picked(x, x_lead, (rows, depth), lambda i: (0, 0)),
            picked(modulation, (0, r), (3, depth), lambda i: (0, 0)),
            pl.BlockSpec((1, LANES), lambda i: (0, 0)),
            pl.BlockSpec((depth, BLOCK), lambda i: (0, i)),
        ],
        out_specs=pl.BlockSpec((rows, BLOCK), lambda i: (0, i)),
        out_shape=jax.ShapeDtypeStruct((rows, columns), jnp.bfloat16),
        scratch_shapes=[pltpu.VMEM((rows, depth), jnp.bfloat16)],
        compiler_params=PARAMS,
        cost_estimate=pl.CostEstimate(
            flops=2 * rows * depth * columns,
            bytes_accessed=2 * (depth * columns + rows * depth + rows * columns),
            transcendentals=0,
        ),
    )(x, modulation, gain_row, w)


def attend_kernel(n_sets, *refs):
    q_ref, out_ref = refs[0], refs[-1]
    sets = [refs[1 + 3 * s : 4 + 3 * s] for s in range(n_sets)]
    query = q_ref[...]
    rows = query.shape[0]
    lane = lax.broadcasted_iota(jnp.int32, (1, LANES), 1)
    low = lane < HEAD
    none = jnp.zeros((), jnp.bfloat16)
    one = jnp.ones((), jnp.bfloat16)
    both = jnp.concatenate([jnp.where(low, query, none), jnp.where(low, none, query)], 0)
    def scores_of(keys):
        return lax.dot_general(
            both, keys[...], (((1,), (1,)), ((), ())), preferred_element_type=jnp.float32
        )

    total = None
    scores = scores_of(sets[0][0])
    for place, (_, value_even, value_odd) in enumerate(sets):
        ahead = scores_of(sets[place + 1][0]) if place + 1 < len(sets) else None
        weights = jnp.exp(scores).astype(jnp.bfloat16)
        held = jnp.concatenate(
            [jnp.where(low, one, value_even[...]), jnp.where(low, value_odd[...], one)], 1
        )
        part = jnp.dot(weights, held, preferred_element_type=jnp.float32)
        total = part if total is None else total + part
        scores = ahead
    even, odd = total[:rows, :LANES], total[rows:, LANES:]
    halves = [pltpu.roll(each, HEAD, 1) / each for each in (even, odd)]
    out_ref[...] = jnp.where(lane < HEAD, halves[0], halves[1]).astype(jnp.bfloat16)


def attend(qkv_out, held_lead, n_query, sets, width):
    rows = qkv_out.shape[-2]
    pairs = n_query // LANES
    own = n_query // LANES
    last = 2 * width // LANES - 1
    first_value = width // LANES

    def specs(array, lead, offset):
        shape = (array.shape[-2], LANES)
        return [
            picked(array, lead, shape, lambda i: (0, offset + i)),
            picked(array, lead, shape, lambda i: (0, offset + first_value + i)),
            picked(
                array,
                lead,
                shape,
                lambda i: (0, offset + jnp.minimum(first_value + 1 + i, last)),
            ),
        ]

    in_specs = [picked(qkv_out, held_lead, (rows, LANES), lambda i: (0, i))]
    operands = [qkv_out]
    for array, lead, offset in [(qkv_out, held_lead, own)] + [pair + (0,) for pair in sets]:
        in_specs += specs(array, lead, offset)
        operands += [array] * 3
    count = rows + sum(array.shape[-2] for array, _ in sets)
    return pl.pallas_call(
        functools.partial(attend_kernel, 1 + len(sets)),
        grid=(pairs,),
        in_specs=in_specs,
        out_specs=pl.BlockSpec((rows, LANES), lambda i: (0, i)),
        out_shape=jax.ShapeDtypeStruct((rows, n_query), jnp.bfloat16),
        compiler_params=PARAMS,
        cost_estimate=pl.CostEstimate(
            flops=16 * rows * count * width,
            bytes_accessed=4 * count * width,
            transcendentals=rows * count * width // HEAD,
        ),
    )(*operands)


def out_kernel(width, x_ref, attn_ref, mod_ref, w_ref, *rest):
    attn = attn_ref[:, :width]
    proj = jnp.concatenate(
        [
            jnp.dot(attn, w_ref[shard], preferred_element_type=jnp.float32)
            for shard in range(w_ref.shape[0])
        ],
        -1,
    )
    x_next = (x_ref[...].astype(jnp.float32) + mod_ref[2:3, :] * proj).astype(jnp.bfloat16)
    if len(rest) == 1:
        rest[0][...] = x_next
        return
    fmod_ref, fw_ref, vel_ref = rest
    final = modulated(x_next.astype(jnp.float32), fmod_ref[0:1, :], fmod_ref[1:2, :])
    vel_ref[...] = jnp.dot(
        final.astype(jnp.bfloat16), fw_ref[...], preferred_element_type=jnp.float32
    )


def project_out(x, x_lead, attn, modulation, r, w, final=None):
    rows, depth = x.shape[-2:]
    width = w.shape[1]
    operands = [x, attn, modulation, w]
    specs = [
        picked(x, x_lead, (rows, depth), lambda i: (0, 0)),
        pl.BlockSpec(attn.shape, lambda i: (0, 0)),
        picked(modulation, (0, r), (3, depth), lambda i: (0, 0)),
        pl.BlockSpec(w.shape, lambda i: (0, 0, 0)),
    ]
    if final is None:
        shape = jax.ShapeDtypeStruct((rows, depth), jnp.bfloat16)
    else:
        operands += list(final)
        specs.append(picked(final[0], (r,), final[0].shape[1:], lambda i: (0, 0)))
        specs.append(pl.BlockSpec(final[1].shape, lambda i: (0, 0)))
        shape = jax.ShapeDtypeStruct((rows, final[1].shape[1]), jnp.float32)
    return pl.pallas_call(
        functools.partial(out_kernel, width),
        grid=(1,),
        in_specs=specs,
        out_specs=pl.BlockSpec(shape.shape, lambda i: (0, 0)),
        out_shape=shape,
        compiler_params=PARAMS,
        cost_estimate=pl.CostEstimate(
            flops=2 * rows * depth * width,
            bytes_accessed=2 * (depth * width + 3 * rows * depth),
            transcendentals=0,
        ),
    )(*operands)


MESH = pl.DeviceIdType.MESH
LAG = 3


def row_chunks(rows):
    first = pl.cdiv(rows // 16, 2) * 16
    return ((0, first), (first, rows - first))


def greet(n, me, patch):
    has_left, has_right = me > 0, me < n - 1
    barrier = pltpu.get_barrier_semaphore()
    for other in (1, 2):
        pl.semaphore_signal(
            barrier, inc=1, device_id={"patch": patch ^ other}, device_id_type=MESH
        )

    @pl.when(has_left)
    def _():
        pl.semaphore_signal(barrier, inc=1, device_id={"shard": me - 1}, device_id_type=MESH)

    @pl.when(has_right)
    def _():
        pl.semaphore_signal(barrier, inc=1, device_id={"shard": me + 1}, device_id_type=MESH)

    pl.semaphore_wait(
        barrier, 2 + jnp.where(has_left, 1, 0) + jnp.where(has_right, 1, 0)
    )


def shard_block(me, way, t):
    return me - t if way == 0 else me + t


def out_copies(wo_ref, wo_all, os_, or_):
    me = lax.axis_index("shard")
    patch = lax.axis_index("patch")
    o_rows = wo_all.shape[1] // 2

    def o_copy(way, t, sending):
        b = shard_block(me, way, t if sending else t + 1)
        half = pl.ds(pl.multiple_of((patch % 2) * o_rows, 16), o_rows)
        dst = wo_all.at[b, half]
        src = wo_ref.at[half] if sending and t == 0 else dst
        return pltpu.make_async_remote_copy(
            src_ref=src,
            dst_ref=dst,
            send_sem=os_.at[0, way, t],
            recv_sem=or_.at[0, way, t],
            device_id={"shard": me + 1 if way == 0 else me - 1},
            device_id_type=MESH,
        )

    def o_hop(way, t, sending):
        parity = patch % 2 if sending else 1 - patch % 2
        place = wo_all.at[
            shard_block(me, way, t + 1), pl.ds(pl.multiple_of(parity * o_rows, 16), o_rows)
        ]
        return pltpu.make_async_remote_copy(
            src_ref=place,
            dst_ref=place,
            send_sem=os_.at[1, way, t],
            recv_sem=or_.at[1, way, t],
            device_id={"patch": patch ^ 1},
            device_id_type=MESH,
        )

    return o_copy, o_hop


def stale_copies(stale_ref, stale_all, ss, sr, first=0):
    patch = lax.axis_index("patch")

    def s_copy(kind, r):
        return pltpu.make_async_remote_copy(
            src_ref=stale_all.at[0, r] if kind == 2 else stale_ref.at[r + first],
            dst_ref=stale_all.at[kind, r],
            send_sem=ss.at[kind, r],
            recv_sem=sr.at[kind, r],
            device_id={"patch": patch ^ (2 if kind == 0 else 1)},
            device_id_type=MESH,
        )

    return s_copy


def gather_kernel(
    n, w_ref, wo_ref, stale_ref, w_all, wo_all, stale_all, own, zs, zr, hs, hr, os_, or_, ss, sr
):
    me = lax.axis_index("shard")
    patch = lax.axis_index("patch")
    rows, columns = w_ref.shape
    half_rows, half_columns = rows // 2, columns // 2
    chunks = row_chunks(half_rows)
    has_left, has_right = me > 0, me < n - 1

    greet(n, me, patch)

    def spot(ref, base, quarter, k):
        start, size = chunks[k]
        return ref.at[
            pl.ds(pl.multiple_of(base + (quarter // 2) * half_rows + start, 16), size),
            pl.ds(pl.multiple_of((quarter % 2) * half_columns, LANES), half_columns),
        ]

    def block(way, t):
        return me - t if way == 0 else me + t

    def incoming(way, t):
        return (me - 1 - t >= 0) if way == 0 else (me + 1 + t < n)

    def ahead(way):
        return has_right if way == 0 else has_left

    def z_copy(way, t, k, sending):
        b = block(way, t if sending else t + 1)
        dst = spot(w_all, b * rows, patch, k)
        src = spot(w_ref, 0, patch, k) if sending and t == 0 else dst
        return pltpu.make_async_remote_copy(
            src_ref=src,
            dst_ref=dst,
            send_sem=zs.at[way, t, k],
            recv_sem=zr.at[way, t, k],
            device_id={"shard": me + 1 if way == 0 else me - 1},
            device_id_type=MESH,
        )

    def hop(kind, way, t, k, sending):
        to = 2 if kind == 0 else 1
        held = patch ^ 2 if kind == 2 else patch
        place = spot(w_all, block(way, t + 1) * rows, held if sending else held ^ to, k)
        return pltpu.make_async_remote_copy(
            src_ref=place,
            dst_ref=place,
            send_sem=hs.at[kind, way, t, k],
            recv_sem=hr.at[kind, way, t, k],
            device_id={"patch": patch ^ to},
            device_id_type=MESH,
        )

    o_copy, o_hop = out_copies(wo_ref, wo_all, os_, or_)

    s_copy = stale_copies(stale_ref, stale_all, ss, sr)

    for way in range(2):

        @pl.when(ahead(way))
        def _(way=way):
            for k in range(len(chunks)):
                z_copy(way, 0, k, True).start()

    s_copy(0, 0).start()
    s_copy(1, 0).start()
    own_w = pltpu.make_async_copy(
        w_ref, w_all.at[pl.ds(pl.multiple_of(me * rows, 16), rows)], own.at[0]
    )
    own_o = pltpu.make_async_copy(wo_ref, wo_all.at[me], own.at[1])
    own_w.start()
    own_o.start()

    items = [
        (way, t, k) for t in range(n - 1) for k in range(len(chunks)) for way in range(2)
    ]

    def pass_on(way, t, k):
        @pl.when(incoming(way, t))
        def _():
            hop(0, way, t, k, False).wait_recv()
            hop(2, way, t, k, True).start()

    for place, (way, t, k) in enumerate(items):

        @pl.when(incoming(way, t))
        def _(way=way, t=t, k=k):
            z_copy(way, t, k, False).wait_recv()
            if t + 1 < n - 1:

                @pl.when(ahead(way))
                def _():
                    z_copy(way, t + 1, k, True).start()

            hop(0, way, t, k, True).start()
            hop(1, way, t, k, True).start()

        if place >= 2 * LAG:
            pass_on(*items[place - 2 * LAG])
        if t == max(n - 3, 0) and k == len(chunks) - 1:

            @pl.when(ahead(way))
            def _(way=way):
                o_copy(way, 0, True).start()

    s_copy(0, 0).wait_recv()
    s_copy(2, 0).start()
    left = items[max(len(items) - 2 * LAG, 0) :]
    for t in range(n - 2):
        for way in range(2):

            @pl.when(incoming(way, t))
            def _(way=way, t=t):
                o_copy(way, t, False).wait_recv()
                if t + 1 < n - 2:

                    @pl.when(ahead(way))
                    def _():
                        o_copy(way, t + 1, True).start()

                o_hop(way, t, True).start()

        share = pl.cdiv(len(left), n - 2)
        for item in left[t * share : (t + 1) * share]:
            pass_on(*item)

    for way, t, k in items:

        @pl.when(incoming(way, t))
        def _(way=way, t=t, k=k):
            for kind in range(3):
                hop(kind, way, t, k, True).wait_send()
            for kind in (1, 2):
                hop(kind, way, t, k, False).wait_recv()

        sends = incoming(way, t - 1) if t > 0 else True

        @pl.when(jnp.logical_and(ahead(way), sends))
        def _(way=way, t=t, k=k):
            z_copy(way, t, k, True).wait_send()

        if k == 0 and t < n - 2:

            @pl.when(incoming(way, t))
            def _(way=way, t=t):
                o_hop(way, t, True).wait_send()
                o_hop(way, t, False).wait_recv()

            @pl.when(jnp.logical_and(ahead(way), sends))
            def _(way=way, t=t):
                o_copy(way, t, True).wait_send()

    for kind in range(3):
        s_copy(kind, 0).wait_send()
    for kind in (1, 2):
        s_copy(kind, 0).wait_recv()
    own_w.wait()
    own_o.wait()


def gather(w, w_out, stale, n):
    rows, columns = w.shape
    anywhere = pl.BlockSpec(memory_space=pl.ANY)
    dma = pltpu.SemaphoreType.DMA
    return pl.pallas_call(
        functools.partial(gather_kernel, n),
        in_specs=[anywhere] * 3,
        out_specs=[anywhere] * 3,
        out_shape=[
            jax.ShapeDtypeStruct((n * rows, columns), w.dtype),
            jax.ShapeDtypeStruct((n,) + w_out.shape, w_out.dtype),
            jax.ShapeDtypeStruct((3, 1) + stale.shape[1:], stale.dtype),
        ],
        scratch_shapes=[
            dma((2,)),
            dma((2, n - 1, 2)),
            dma((2, n - 1, 2)),
            dma((3, 2, n - 1, 2)),
            dma((3, 2, n - 1, 2)),
            dma((2, 2, n - 2)),
            dma((2, 2, n - 2)),
            dma((3, 1)),
            dma((3, 1)),
        ],
        compiler_params=pltpu.CompilerParams(
            collective_id=0, has_side_effects=True, vmem_limit_bytes=56 * 1024 * 1024
        ),
        cost_estimate=pl.CostEstimate(
            flops=0, bytes_accessed=4 * n * rows * columns, transcendentals=0
        ),
    )(w, w_out, stale)


def first_kernel(
    n, n_query, n_key, x_ref, mod_ref, gain_ref, w_ref, stale_ref, wo_in, out_ref, wo_all,
    stale_all, normed_ref, os_, or_, ss, sr,
):
    step = pl.program_id(1)
    at = pl.program_id(0) * pl.num_programs(1) + step
    last = pl.num_programs(0) * pl.num_programs(1) - 1
    me = lax.axis_index("shard")
    o_copy, o_hop = out_copies(None, wo_all, os_, or_)
    s_copy = stale_copies(stale_ref, stale_all, ss, sr, 1)
    others = stale_all.shape[1]
    ends = (me == n - 1, me == 0)
    before = (me == n - 2, me == 1)

    @pl.when(at == 0)
    def _():
        greet(n, me, lax.axis_index("patch"))
        for way in range(2):

            @pl.when(before[way])
            def _(way=way):
                o_copy(way, n - 2, True).start()

        for r in range(others):
            s_copy(0, r).start()
            s_copy(1, r).start()

    qkv_step(step, n_query, n_key, x_ref, mod_ref, gain_ref, w_ref, out_ref, normed_ref)

    @pl.when(at == last - 1)
    def _():
        for way in range(2):

            @pl.when(ends[way])
            def _(way=way):
                o_copy(way, n - 2, False).wait_recv()
                o_hop(way, n - 2, True).start()

        for r in range(others):
            s_copy(0, r).wait_recv()
            s_copy(2, r).start()

    @pl.when(at == last)
    def _():
        for way in range(2):

            @pl.when(before[way])
            def _(way=way):
                o_copy(way, n - 2, True).wait_send()

            @pl.when(ends[way])
            def _(way=way):
                o_hop(way, n - 2, True).wait_send()
                o_hop(way, n - 2, False).wait_recv()

        for r in range(others):
            for kind in range(3):
                s_copy(kind, r).wait_send()
            for kind in (1, 2):
                s_copy(kind, r).wait_recv()


def first_qkv(x, modulation, gain, w, stale, wo_all, n, n_query, n_key):
    requests, rows, depth = x.shape
    columns = w.shape[1]
    gain_row = jnp.tile(gain / math.sqrt(HEAD), LANES // HEAD)[None]
    anywhere = pl.BlockSpec(memory_space=pl.ANY)
    dma = pltpu.SemaphoreType.DMA
    others = requests - 1
    return pl.pallas_call(
        functools.partial(first_kernel, n, n_query, n_key),
        grid=(requests, pl.cdiv(columns, BLOCK)),
        in_specs=[
            pl.BlockSpec((None, rows, depth), lambda r, i: (r, 0, 0)),
            pl.BlockSpec((None, None, 3, depth), lambda r, i: (0, r, 0, 0)),
            pl.BlockSpec((1, LANES), lambda r, i: (0, 0)),
            pl.BlockSpec((depth, BLOCK), lambda r, i: (0, i)),
            anywhere,
            anywhere,
        ],
        out_specs=[
            pl.BlockSpec((None, rows, BLOCK), lambda r, i: (r, 0, i)),
            anywhere,
            anywhere,
        ],
        out_shape=[
            jax.ShapeDtypeStruct((requests, rows, columns), jnp.bfloat16),
            jax.ShapeDtypeStruct(wo_all.shape, wo_all.dtype),
            jax.ShapeDtypeStruct((3, others) + stale.shape[1:], stale.dtype),
        ],
        scratch_shapes=[
            pltpu.VMEM((rows, depth), jnp.bfloat16),
            dma((2, 2, n - 1)),
            dma((2, 2, n - 1)),
            dma((3, others)),
            dma((3, others)),
        ],
        input_output_aliases={5: 1},
        compiler_params=pltpu.CompilerParams(
            collective_id=1, has_side_effects=True, vmem_limit_bytes=56 * 1024 * 1024
        ),
        cost_estimate=pl.CostEstimate(
            flops=2 * requests * rows * depth * columns,
            bytes_accessed=2 * depth * columns * requests,
            transcendentals=0,
        ),
    )(x, modulation, gain_row, w, stale, wo_all)


def on_device(
    hidden,
    text_kv,
    stale_kv,
    modulation,
    score_gain,
    qkv_weight,
    out_weight,
    final_mod,
    final_weight,
    latent,
    step_index,
):
    section = lax.axis_index("section")
    patch = lax.axis_index("patch")
    patches = lax.axis_size("patch")
    shards = lax.axis_size("shard")
    requests, rows, depth = hidden.shape
    width = out_weight.shape[1]
    n_query = pl.cdiv(width, LANES) * LANES

    columns = pl.cdiv(n_query + 2 * width, 2 * LANES) * 2 * LANES
    w = qkv_weight[0]
    packed = pack(w, width, n_query, columns)
    if patches == 4 and shards > 2 and requests > 1 and w.shape[0] % 32 == 0 and width % 32 == 0:
        w_qkv, w_out, stale_first = gather(packed, out_weight[0], stale_kv[0], shards)
        held, w_out, stale_rest = first_qkv(
            hidden, modulation, score_gain[0], w_qkv, stale_kv[0], w_out, shards, n_query, width
        )
        helds = [(held, (r,)) for r in range(requests)]
        stale = [
            [(stale_rest, (i, r - 1)) if r else (stale_first, (i, 0)) for i in range(3)]
            for r in range(requests)
        ]
    else:
        share = w.shape[0] // patches
        mine = lax.dynamic_slice_in_dim(packed, patch * share, share, 0)
        w_qkv = lax.all_gather(mine, ("shard", "patch"), axis=0, tiled=True)
        share = width // patches
        mine = lax.dynamic_slice_in_dim(out_weight[0], patch * share, share, 0)
        w_out = lax.all_gather(mine, ("shard", "patch"), axis=0, tiled=True)
        w_out = w_out.reshape(shards, width, out_weight.shape[2])
        stale = [stale_kv[0]]
        step = patches // 2
        while step >= 1:
            pairs = [(p, p ^ step) for p in range(patches)]
            stale = stale + [lax.ppermute(array, "patch", pairs) for array in stale]
            step //= 2
        stale = [[(array, (r,)) for array in stale[1:]] for r in range(requests)]
        helds = [
            (qkv(hidden, (r,), modulation, r, score_gain[0], w_qkv, n_query, width), ())
            for r in range(requests)
        ]

    def after(r, x, x_lead, held, held_lead, final=None):
        attn = attend(held, held_lead, n_query, stale[r] + [(text_kv, (0, r))], width)
        return project_out(x, x_lead, attn, modulation, r, w_out, final)

    hop = [(s, s + 1) for s in range(lax.axis_size("section") - 1)]
    arrived, velocity, lasts = [], [], []
    for r in range(requests):
        x_next = after(r, hidden, (r,), *helds[r])
        arrived.append(lax.ppermute(x_next, "section", hop))
    for r in range(requests):
        held = qkv(arrived[r], (), modulation, r, score_gain[0], w_qkv, n_query, width)
        lasts.append((held, ()))
        velocity.append(after(r, arrived[r], (), held, (), (final_mod, final_weight)))
    fresh = jnp.stack(
        [
            jnp.where(section == 0, early[lead], late[late_lead])[
                :, n_query : n_query + 2 * width
            ]
            for (early, lead), (late, late_lead) in zip(helds, lasts)
        ]
    )
    velocity = jnp.stack(velocity)
    half = latent.shape[1]
    back = lax.ppermute(velocity[:, :half].astype(jnp.bfloat16), "section", [(1, 0)])
    velocity_mine = jnp.where(section == 0, back.astype(jnp.float32), velocity[:, half:])
    sig = sigma_of(step_index)[:, None, None]
    sig_next = sigma_of(step_index + 1)[:, None, None]
    latent_next = latent + (sig_next - sig) * velocity_mine
    denoised = latent - sig * velocity_mine
    return (fresh[None], latent_next, denoised)


def solution(mesh):
    in_specs = (
        P("shard", "patch", None),
        P("section", "shard", None, None),
        P("section", "shard", "patch", None),
        P("section", "shard", None, None),
        P("section", None),
        P("section", "shard", None),
        P("section", None, "shard"),
        P("shard", None, None),
        P(),
        P("shard", ("patch", "section"), None),
        P("shard"),
    )
    out_specs = (
        P("section", "shard", "patch", None),
        P("shard", ("patch", "section"), None),
        P("shard", ("patch", "section"), None),
    )
    return jax.shard_map(
        on_device, mesh=mesh, in_specs=in_specs, out_specs=out_specs, check_vma=False
    )
```

```python
import functools
import math

import jax
import jax.numpy as jnp
from jax import lax
from jax.experimental import pallas as pl
from jax.experimental.pallas import tpu as pltpu
from jax.sharding import PartitionSpec as P

HEAD = 64
NSTEPS = 28
LANES = 128
BLOCK = 768

eps_norm = 1e-06
flow_shift = 3.0

PARAMS = pltpu.CompilerParams(vmem_limit_bytes=56 * 1024 * 1024)


def sigma_of(step):
    s = 1.0 - step.astype(jnp.float32) / NSTEPS
    return flow_shift * s / (1.0 + (flow_shift - 1.0) * s)


def modulated(xf, shift, scale):
    mean = jnp.mean(xf, -1, keepdims=True)
    cent = xf - mean
    var = jnp.mean(cent * cent, -1, keepdims=True)
    return cent * lax.rsqrt(var + eps_norm) * (1.0 + scale) + shift


def head_means(squares):
    row = lax.broadcasted_iota(jnp.int32, (LANES, LANES), 0) // HEAD
    col = lax.broadcasted_iota(jnp.int32, (LANES, LANES), 1) // HEAD
    same = jnp.where(row == col, 1.0 / HEAD, 0.0).astype(jnp.bfloat16)
    high = squares.astype(jnp.bfloat16)
    low = (squares - high.astype(jnp.float32)).astype(jnp.bfloat16)
    return jnp.dot(high, same, preferred_element_type=jnp.float32) + jnp.dot(
        low, same, preferred_element_type=jnp.float32
    )


def qkv_kernel(n_query, n_key, x_ref, mod_ref, gain_ref, w_ref, out_ref, normed_ref):
    qkv_step(pl.program_id(0), n_query, n_key, x_ref, mod_ref, gain_ref, w_ref, out_ref, normed_ref)


def qkv_step(step, n_query, n_key, x_ref, mod_ref, gain_ref, w_ref, out_ref, normed_ref):
    @pl.when(step == 0)
    def _():
        xf = x_ref[...].astype(jnp.float32)
        normed_ref[...] = modulated(xf, mod_ref[0:1, :], mod_ref[1:2, :]).astype(jnp.bfloat16)

    proj = jnp.dot(normed_ref[...], w_ref[...], preferred_element_type=jnp.float32)
    for low in range(0, BLOCK, LANES):
        part = proj[:, low : low + LANES]
        col = step * BLOCK + low + lax.broadcasted_iota(jnp.int32, (1, LANES), 1)
        factor = lax.rsqrt(head_means(part * part) + eps_norm)
        scaled = part * factor * jnp.where(col < n_query, gain_ref[...], 1.0)
        out_ref[:, low : low + LANES] = jnp.where(col < n_query + n_key, scaled, part).astype(
            jnp.bfloat16
        )


def pack_kernel(width, n_query, w_ref, out_ref):
    out_ref[...] = jnp.zeros_like(out_ref)
    out_ref[:, :width] = w_ref[:, :width]
    out_ref[:, n_query : n_query + 2 * width] = w_ref[:, width:]


def pack(w, width, n_query, columns):
    rows = w.shape[0]
    block = min(rows, 160)
    return pl.pallas_call(
        functools.partial(pack_kernel, width, n_query),
        grid=(pl.cdiv(rows, block),),
        in_specs=[pl.BlockSpec((block, w.shape[1]), lambda i: (i, 0))],
        out_specs=pl.BlockSpec((block, columns), lambda i: (i, 0)),
        out_shape=jax.ShapeDtypeStruct((rows, columns), w.dtype),
        compiler_params=PARAMS,
    )(w)


def picked(array, lead, shape, index):
    return pl.BlockSpec(
        (None,) * len(lead) + shape, lambda *grid: tuple(lead) + tuple(index(*grid))
    )


def qkv(x, x_lead, modulation, r, gain, w, n_query, n_key):
    rows, depth = x.shape[-2:]
    columns = w.shape[1]
    gain_row = jnp.tile(gain / math.sqrt(HEAD), LANES // HEAD)[None]
    return pl.pallas_call(
        functools.partial(qkv_kernel, n_query, n_key),
        grid=(pl.cdiv(columns, BLOCK),),
        in_specs=[
            picked(x, x_lead, (rows, depth), lambda i: (0, 0)),
            picked(modulation, (0, r), (3, depth), lambda i: (0, 0)),
            pl.BlockSpec((1, LANES), lambda i: (0, 0)),
            pl.BlockSpec((depth, BLOCK), lambda i: (0, i)),
        ],
        out_specs=pl.BlockSpec((rows, BLOCK), lambda i: (0, i)),
        out_shape=jax.ShapeDtypeStruct((rows, columns), jnp.bfloat16),
        scratch_shapes=[pltpu.VMEM((rows, depth), jnp.bfloat16)],
        compiler_params=PARAMS,
        cost_estimate=pl.CostEstimate(
            flops=2 * rows * depth * columns,
            bytes_accessed=2 * (depth * columns + rows * depth + rows * columns),
            transcendentals=0,
        ),
    )(x, modulation, gain_row, w)


def attend_kernel(n_sets, *refs):
    q_ref, out_ref = refs[0], refs[-1]
    sets = [refs[1 + 3 * s : 4 + 3 * s] for s in range(n_sets)]
    query = q_ref[...]
    rows = query.shape[0]
    lane = lax.broadcasted_iota(jnp.int32, (1, LANES), 1)
    low = lane < HEAD
    none = jnp.zeros((), jnp.bfloat16)
    one = jnp.ones((), jnp.bfloat16)
    both = jnp.concatenate([jnp.where(low, query, none), jnp.where(low, none, query)], 0)
    def scores_of(keys):
        return lax.dot_general(
            both, keys[...], (((1,), (1,)), ((), ())), preferred_element_type=jnp.float32
        )

    total = None
    scores = scores_of(sets[0][0])
    for place, (_, value_even, value_odd) in enumerate(sets):
        ahead = scores_of(sets[place + 1][0]) if place + 1 < len(sets) else None
        weights = jnp.exp(scores).astype(jnp.bfloat16)
        held = jnp.concatenate(
            [jnp.where(low, one, value_even[...]), jnp.where(low, value_odd[...], one)], 1
        )
        part = jnp.dot(weights, held, preferred_element_type=jnp.float32)
        total = part if total is None else total + part
        scores = ahead
    even, odd = total[:rows, :LANES], total[rows:, LANES:]
    halves = [pltpu.roll(each, HEAD, 1) / each for each in (even, odd)]
    out_ref[...] = jnp.where(lane < HEAD, halves[0], halves[1]).astype(jnp.bfloat16)


def attend(qkv_out, held_lead, n_query, sets, width):
    rows = qkv_out.shape[-2]
    pairs = n_query // LANES
    own = n_query // LANES
    last = 2 * width // LANES - 1
    first_value = width // LANES

    def specs(array, lead, offset):
        shape = (array.shape[-2], LANES)
        return [
            picked(array, lead, shape, lambda i: (0, offset + i)),
            picked(array, lead, shape, lambda i: (0, offset + first_value + i)),
            picked(
                array,
                lead,
                shape,
                lambda i: (0, offset + jnp.minimum(first_value + 1 + i, last)),
            ),
        ]

    in_specs = [picked(qkv_out, held_lead, (rows, LANES), lambda i: (0, i))]
    operands = [qkv_out]
    for array, lead, offset in [(qkv_out, held_lead, own)] + [pair + (0,) for pair in sets]:
        in_specs += specs(array, lead, offset)
        operands += [array] * 3
    count = rows + sum(array.shape[-2] for array, _ in sets)
    return pl.pallas_call(
        functools.partial(attend_kernel, 1 + len(sets)),
        grid=(pairs,),
        in_specs=in_specs,
        out_specs=pl.BlockSpec((rows, LANES), lambda i: (0, i)),
        out_shape=jax.ShapeDtypeStruct((rows, n_query), jnp.bfloat16),
        compiler_params=PARAMS,
        cost_estimate=pl.CostEstimate(
            flops=16 * rows * count * width,
            bytes_accessed=4 * count * width,
            transcendentals=rows * count * width // HEAD,
        ),
    )(*operands)


def out_kernel(width, x_ref, attn_ref, mod_ref, w_ref, *rest):
    attn = attn_ref[:, :width]
    proj = jnp.concatenate(
        [
            jnp.dot(attn, w_ref[shard], preferred_element_type=jnp.float32)
            for shard in range(w_ref.shape[0])
        ],
        -1,
    )
    x_next = (x_ref[...].astype(jnp.float32) + mod_ref[2:3, :] * proj).astype(jnp.bfloat16)
    if len(rest) == 1:
        rest[0][...] = x_next
        return
    fmod_ref, fw_ref, vel_ref = rest
    final = modulated(x_next.astype(jnp.float32), fmod_ref[0:1, :], fmod_ref[1:2, :])
    vel_ref[...] = jnp.dot(
        final.astype(jnp.bfloat16), fw_ref[...], preferred_element_type=jnp.float32
    )


def project_out(x, x_lead, attn, modulation, r, w, final=None):
    rows, depth = x.shape[-2:]
    width = w.shape[1]
    operands = [x, attn, modulation, w]
    specs = [
        picked(x, x_lead, (rows, depth), lambda i: (0, 0)),
        pl.BlockSpec(attn.shape, lambda i: (0, 0)),
        picked(modulation, (0, r), (3, depth), lambda i: (0, 0)),
        pl.BlockSpec(w.shape, lambda i: (0, 0, 0)),
    ]
    if final is None:
        shape = jax.ShapeDtypeStruct((rows, depth), jnp.bfloat16)
    else:
        operands += list(final)
        specs.append(picked(final[0], (r,), final[0].shape[1:], lambda i: (0, 0)))
        specs.append(pl.BlockSpec(final[1].shape, lambda i: (0, 0)))
        shape = jax.ShapeDtypeStruct((rows, final[1].shape[1]), jnp.float32)
    return pl.pallas_call(
        functools.partial(out_kernel, width),
        grid=(1,),
        in_specs=specs,
        out_specs=pl.BlockSpec(shape.shape, lambda i: (0, 0)),
        out_shape=shape,
        compiler_params=PARAMS,
        cost_estimate=pl.CostEstimate(
            flops=2 * rows * depth * width,
            bytes_accessed=2 * (depth * width + 3 * rows * depth),
            transcendentals=0,
        ),
    )(*operands)


MESH = pl.DeviceIdType.MESH
LAG = 3


def row_pieces(rows, shared):
    if not shared:
        return ((0, rows // 2, rows // 2, True),)
    own = rows * 27 // 64 // 32 * 32
    half = own // 2
    return (
        (0, rows - own, half, True),
        (half, rows - half, half, True),
        (own, own, rows - 2 * own, False),
    )


def greet(n, me, patch):
    has_left, has_right = me > 0, me < n - 1
    barrier = pltpu.get_barrier_semaphore()
    for other in (1, 2):
        pl.semaphore_signal(
            barrier, inc=1, device_id={"patch": patch ^ other}, device_id_type=MESH
        )

    @pl.when(has_left)
    def _():
        pl.semaphore_signal(barrier, inc=1, device_id={"shard": me - 1}, device_id_type=MESH)

    @pl.when(has_right)
    def _():
        pl.semaphore_signal(barrier, inc=1, device_id={"shard": me + 1}, device_id_type=MESH)

    pl.semaphore_wait(
        barrier, 2 + jnp.where(has_left, 1, 0) + jnp.where(has_right, 1, 0)
    )


def shard_block(me, way, t):
    return me - t if way == 0 else me + t


def relay(w_ref, spot, zs, zr, hs, hr):
    me = lax.axis_index("shard")
    patch = lax.axis_index("patch")

    def z_copy(way, t, k, sending):
        b = shard_block(me, way, t if sending else t + 1)
        dst = spot(None, b, patch, k)
        src = spot(w_ref, None, patch, k) if sending and t == 0 else dst
        return pltpu.make_async_remote_copy(
            src_ref=src,
            dst_ref=dst,
            send_sem=zs.at[way, t, k],
            recv_sem=zr.at[way, t, k],
            device_id={"shard": me + 1 if way == 0 else me - 1},
            device_id_type=MESH,
        )

    def hop(kind, way, t, k, sending):
        to = 2 if kind == 0 else 1
        held = patch ^ 2 if kind == 2 else patch
        place = spot(None, shard_block(me, way, t + 1), held if sending else held ^ to, k)
        return pltpu.make_async_remote_copy(
            src_ref=place,
            dst_ref=place,
            send_sem=hs.at[kind, way, t, k],
            recv_sem=hr.at[kind, way, t, k],
            device_id={"patch": patch ^ to},
            device_id_type=MESH,
        )

    return z_copy, hop


class Gather:
    def __init__(self, n, pieces, z_copy, hop):
        self.n, self.pieces, self.z_copy, self.hop = n, pieces, z_copy, hop
        self.me = lax.axis_index("shard")
        self.items = [
            (way, t, k) for t in range(n - 1) for k in range(len(pieces)) for way in range(2)
        ]

    def incoming(self, way, t):
        return (self.me - 1 - t >= 0) if way == 0 else (self.me + 1 + t < self.n)

    def ahead(self, way):
        return self.me < self.n - 1 if way == 0 else self.me > 0

    def begin(self):
        for way in range(2):

            @pl.when(self.ahead(way))
            def _(way=way):
                for k in range(len(self.pieces)):
                    self.z_copy(way, 0, k, True).start()

    def arrive(self, way, t, k):
        @pl.when(self.incoming(way, t))
        def _():
            self.z_copy(way, t, k, False).wait_recv()
            if t + 1 < self.n - 1:

                @pl.when(self.ahead(way))
                def _():
                    self.z_copy(way, t + 1, k, True).start()

            if self.pieces[k][3]:
                self.hop(0, way, t, k, True).start()
            self.hop(1, way, t, k, True).start()

    def pass_on(self, way, t, k):
        if self.pieces[k][3]:

            @pl.when(self.incoming(way, t))
            def _():
                self.hop(0, way, t, k, False).wait_recv()
                self.hop(2, way, t, k, True).start()

    def finish(self):
        for way, t, k in self.items:
            kinds = (0, 1, 2) if self.pieces[k][3] else (1,)

            @pl.when(self.incoming(way, t))
            def _(way=way, t=t, k=k, kinds=kinds):
                for kind in kinds:
                    self.hop(kind, way, t, k, True).wait_send()
                for kind in kinds:
                    if kind:
                        self.hop(kind, way, t, k, False).wait_recv()

            sends = self.incoming(way, t - 1) if t > 0 else True

            @pl.when(jnp.logical_and(self.ahead(way), sends))
            def _(way=way, t=t, k=k):
                self.z_copy(way, t, k, True).wait_send()


def gather_kernel(n, w_ref, stale_ref, w_all, stale_all, beside, own, zs, zr, hs, hr, ss, sr):
    me = lax.axis_index("shard")
    patch = lax.axis_index("patch")
    rows, columns = w_ref.shape
    half_columns = columns // 2
    pieces = row_pieces(rows, True)
    greet(n, me, patch)

    def spot(ref, shard, quarter, k):
        early, late, size, _ = pieces[k]
        base = 0 if shard is None else shard * rows
        start = base + jnp.where(quarter // 2 == 0, early, late)
        return (w_all if ref is None else ref).at[
            pl.ds(pl.multiple_of(start, 16), size),
            pl.ds(pl.multiple_of((quarter % 2) * half_columns, LANES), half_columns),
        ]

    def s_copy(kind):
        src = (stale_ref.at[0], stale_ref.at[0], stale_all.at[0], stale_ref.at[pl.ds(1, others)])
        return pltpu.make_async_remote_copy(
            src_ref=src[kind],
            dst_ref=beside if kind == 3 else stale_all.at[kind],
            send_sem=ss.at[kind],
            recv_sem=sr.at[kind],
            device_id={"patch": patch ^ (2 if kind == 0 else 1)},
            device_id_type=MESH,
        )

    others = beside.shape[0]
    steps = Gather(n, pieces, *relay(w_ref, spot, zs, zr, hs, hr))
    steps.begin()
    for kind in (0, 1, 3):
        s_copy(kind).start()
    own_w = pltpu.make_async_copy(
        w_ref, w_all.at[pl.ds(pl.multiple_of(me * rows, 16), rows)], own
    )
    own_w.start()
    lag = 2 * LAG
    for place, item in enumerate(steps.items):
        steps.arrive(*item)
        if place >= lag:
            steps.pass_on(*steps.items[place - lag])
    s_copy(0).wait_recv()
    s_copy(2).start()
    for item in steps.items[max(len(steps.items) - lag, 0) :]:
        steps.pass_on(*item)
    steps.finish()
    for kind in range(4):
        s_copy(kind).wait_send()
    for kind in (1, 2, 3):
        s_copy(kind).wait_recv()
    own_w.wait()


def gather(w, stale, n):
    rows, columns = w.shape
    anywhere = pl.BlockSpec(memory_space=pl.ANY)
    dma = pltpu.SemaphoreType.DMA
    return pl.pallas_call(
        functools.partial(gather_kernel, n),
        in_specs=[anywhere] * 2,
        out_specs=[anywhere] * 3,
        out_shape=[
            jax.ShapeDtypeStruct((n * rows, columns), w.dtype),
            jax.ShapeDtypeStruct((3,) + stale.shape[1:], stale.dtype),
            jax.ShapeDtypeStruct((stale.shape[0] - 1,) + stale.shape[1:], stale.dtype),
        ],
        scratch_shapes=[
            dma,
            dma((2, n - 1, 3)),
            dma((2, n - 1, 3)),
            dma((3, 2, n - 1, 3)),
            dma((3, 2, n - 1, 3)),
            dma((4,)),
            dma((4,)),
        ],
        compiler_params=pltpu.CompilerParams(
            collective_id=0, has_side_effects=True, vmem_limit_bytes=56 * 1024 * 1024
        ),
        cost_estimate=pl.CostEstimate(
            flops=0, bytes_accessed=4 * n * rows * columns, transcendentals=0
        ),
    )(w, stale)


def first_kernel(
    n, total, n_query, n_key, x_ref, mod_ref, gain_ref, w_ref, wo_ref, out_ref, wo_all,
    normed_ref, own, zs, zr, hs, hr,
):
    step = pl.program_id(1)
    at = pl.program_id(0) * pl.num_programs(1) + step
    me = lax.axis_index("shard")
    pieces = row_pieces(wo_ref.shape[0], False)

    def spot(ref, shard, quarter, k):
        place = wo_all.at[shard] if ref is None else ref
        size = pieces[k][2] // 2
        return place.at[pl.ds(pl.multiple_of(quarter * size, 16), size)]

    steps = Gather(n, pieces, *relay(wo_ref, spot, zs, zr, hs, hr))
    own_o = pltpu.make_async_copy(wo_ref, wo_all.at[me], own)

    @pl.when(at == 0)
    def _():
        greet(n, me, lax.axis_index("patch"))
        steps.begin()
        own_o.start()

    qkv_step(step, n_query, n_key, x_ref, mod_ref, gain_ref, w_ref, out_ref, normed_ref)

    hooks = [min(total * (t + 1) // (n - 1), total - 2) for t in range(n - 1)]
    for t in range(n - 1):

        @pl.when(at == hooks[t])
        def _(t=t):
            for way in range(2):
                steps.arrive(way, t, 0)
                if t > 0:
                    steps.pass_on(way, t - 1, 0)

    @pl.when(at == total - 1)
    def _():
        for way in range(2):
            steps.pass_on(way, n - 2, 0)
        steps.finish()
        own_o.wait()


def first_qkv(x, modulation, gain, w, w_out, n, n_query, n_key):
    requests, rows, depth = x.shape
    columns = w.shape[1]
    gain_row = jnp.tile(gain / math.sqrt(HEAD), LANES // HEAD)[None]
    anywhere = pl.BlockSpec(memory_space=pl.ANY)
    dma = pltpu.SemaphoreType.DMA
    blocks = pl.cdiv(columns, BLOCK)
    return pl.pallas_call(
        functools.partial(first_kernel, n, requests * blocks, n_query, n_key),
        grid=(requests, blocks),
        in_specs=[
            pl.BlockSpec((None, rows, depth), lambda r, i: (r, 0, 0)),
            pl.BlockSpec((None, None, 3, depth), lambda r, i: (0, r, 0, 0)),
            pl.BlockSpec((1, LANES), lambda r, i: (0, 0)),
            pl.BlockSpec((depth, BLOCK), lambda r, i: (0, i)),
            anywhere,
        ],
        out_specs=[pl.BlockSpec((None, rows, BLOCK), lambda r, i: (r, 0, i)), anywhere],
        out_shape=[
            jax.ShapeDtypeStruct((requests, rows, columns), jnp.bfloat16),
            jax.ShapeDtypeStruct((n,) + w_out.shape, w_out.dtype),
        ],
        scratch_shapes=[
            pltpu.VMEM((rows, depth), jnp.bfloat16),
            dma,
            dma((2, n - 1, 1)),
            dma((2, n - 1, 1)),
            dma((3, 2, n - 1, 1)),
            dma((3, 2, n - 1, 1)),
        ],
        compiler_params=pltpu.CompilerParams(
            collective_id=1, has_side_effects=True, vmem_limit_bytes=56 * 1024 * 1024
        ),
        cost_estimate=pl.CostEstimate(
            flops=2 * requests * rows * depth * columns,
            bytes_accessed=2 * depth * columns * requests,
            transcendentals=0,
        ),
    )(x, modulation, gain_row, w, w_out)


def on_device(
    hidden,
    text_kv,
    stale_kv,
    modulation,
    score_gain,
    qkv_weight,
    out_weight,
    final_mod,
    final_weight,
    latent,
    step_index,
):
    section = lax.axis_index("section")
    patch = lax.axis_index("patch")
    patches = lax.axis_size("patch")
    shards = lax.axis_size("shard")
    requests, rows, depth = hidden.shape
    width = out_weight.shape[1]
    n_query = pl.cdiv(width, LANES) * LANES

    columns = pl.cdiv(n_query + 2 * width, 2 * LANES) * 2 * LANES
    w = qkv_weight[0]
    packed = pack(w, width, n_query, columns)
    if patches == 4 and shards > 2 and requests > 1 and w.shape[0] % 32 == 0 and width % 64 == 0:
        w_qkv, stale_first, beside = gather(packed, stale_kv[0], shards)
        w_qkv, later = lax.optimization_barrier((w_qkv, stale_kv[0, 1:]))
        across = lax.ppermute(later, "patch", [(p, p ^ 2) for p in range(patches)])
        held, w_out = first_qkv(
            hidden, modulation, score_gain[0], w_qkv, out_weight[0], shards, n_query, width
        )
        helds = [(held, (r,)) for r in range(requests)]
        pending = (across, beside)
        stale = [[(stale_first, (i,)) for i in range(3)]]
    else:
        share = w.shape[0] // patches
        mine = lax.dynamic_slice_in_dim(packed, patch * share, share, 0)
        w_qkv = lax.all_gather(mine, ("shard", "patch"), axis=0, tiled=True)
        share = width // patches
        mine = lax.dynamic_slice_in_dim(out_weight[0], patch * share, share, 0)
        w_out = lax.all_gather(mine, ("shard", "patch"), axis=0, tiled=True)
        w_out = w_out.reshape(shards, width, out_weight.shape[2])
        stale = [stale_kv[0]]
        step = patches // 2
        while step >= 1:
            pairs = [(p, p ^ step) for p in range(patches)]
            stale = stale + [lax.ppermute(array, "patch", pairs) for array in stale]
            step //= 2
        stale = [[(array, (r,)) for array in stale[1:]] for r in range(requests)]
        pending = None
        helds = [
            (qkv(hidden, (r,), modulation, r, score_gain[0], w_qkv, n_query, width), ())
            for r in range(requests)
        ]

    def after(r, x, x_lead, held, held_lead, final=None):
        attn = attend(held, held_lead, n_query, stale[r] + [(text_kv, (0, r))], width)
        if len(stale) < requests:
            attn, across = lax.optimization_barrier((attn, pending[0]))
            both = lax.ppermute(across, "patch", [(p, p ^ 1) for p in range(patches)])
            stale.extend(
                [(array, (i,)) for array in (across, pending[1], both)]
                for i in range(requests - 1)
            )
        return project_out(x, x_lead, attn, modulation, r, w_out, final)

    hop = [(s, s + 1) for s in range(lax.axis_size("section") - 1)]
    arrived, velocity, lasts = [], [], []
    for r in range(requests):
        x_next = after(r, hidden, (r,), *helds[r])
        arrived.append(lax.ppermute(x_next, "section", hop))
    arrived = [lax.optimization_barrier((x, x_next))[0] for x in arrived[:-1]] + arrived[-1:]
    for r in range(requests):
        held = qkv(arrived[r], (), modulation, r, score_gain[0], w_qkv, n_query, width)
        lasts.append((held, ()))
        velocity.append(after(r, arrived[r], (), held, (), (final_mod, final_weight)))
    fresh = jnp.stack(
        [
            jnp.where(section == 0, early[lead], late[late_lead])[
                :, n_query : n_query + 2 * width
            ]
            for (early, lead), (late, late_lead) in zip(helds, lasts)
        ]
    )
    velocity = jnp.stack(velocity)
    half = latent.shape[1]
    back = lax.ppermute(velocity[:, :half].astype(jnp.bfloat16), "section", [(1, 0)])
    velocity_mine = jnp.where(section == 0, back.astype(jnp.float32), velocity[:, half:])
    sig = sigma_of(step_index)[:, None, None]
    sig_next = sigma_of(step_index + 1)[:, None, None]
    latent_next = latent + (sig_next - sig) * velocity_mine
    denoised = latent - sig * velocity_mine
    return (fresh[None], latent_next, denoised)


def solution(mesh):
    in_specs = (
        P("shard", "patch", None),
        P("section", "shard", None, None),
        P("section", "shard", "patch", None),
        P("section", "shard", None, None),
        P("section", None),
        P("section", "shard", None),
        P("section", None, "shard"),
        P("shard", None, None),
        P(),
        P("shard", ("patch", "section"), None),
        P("shard"),
    )
    out_specs = (
        P("section", "shard", "patch", None),
        P("shard", ("patch", "section"), None),
        P("shard", ("patch", "section"), None),
    )
    return jax.shard_map(
        on_device, mesh=mesh, in_specs=in_specs, out_specs=out_specs, check_vma=False
    )
```

```python
import functools
import math

import jax
import jax.numpy as jnp
from jax import lax
from jax.experimental import pallas as pl
from jax.experimental.pallas import tpu as pltpu
from jax.sharding import PartitionSpec as P

HEAD = 64
NSTEPS = 28
LANES = 128
BLOCK = 768

eps_norm = 1e-06
flow_shift = 3.0

PARAMS = pltpu.CompilerParams(vmem_limit_bytes=56 * 1024 * 1024)


def sigma_of(step):
    s = 1.0 - step.astype(jnp.float32) / NSTEPS
    return flow_shift * s / (1.0 + (flow_shift - 1.0) * s)


def modulated(xf, shift, scale):
    mean = jnp.mean(xf, -1, keepdims=True)
    cent = xf - mean
    var = jnp.mean(cent * cent, -1, keepdims=True)
    return cent * lax.rsqrt(var + eps_norm) * (1.0 + scale) + shift


def head_means(squares):
    row = lax.broadcasted_iota(jnp.int32, (LANES, LANES), 0) // HEAD
    col = lax.broadcasted_iota(jnp.int32, (LANES, LANES), 1) // HEAD
    same = jnp.where(row == col, 1.0 / HEAD, 0.0).astype(jnp.bfloat16)
    high = squares.astype(jnp.bfloat16)
    low = (squares - high.astype(jnp.float32)).astype(jnp.bfloat16)
    return jnp.dot(high, same, preferred_element_type=jnp.float32) + jnp.dot(
        low, same, preferred_element_type=jnp.float32
    )


def qkv_kernel(n_query, n_key, x_ref, mod_ref, gain_ref, w_ref, out_ref, normed_ref):
    qkv_step(pl.program_id(0), n_query, n_key, x_ref, mod_ref, gain_ref, w_ref, out_ref, normed_ref)


def qkv_step(step, n_query, n_key, x_ref, mod_ref, gain_ref, w_ref, out_ref, normed_ref):
    @pl.when(step == 0)
    def _():
        xf = x_ref[...].astype(jnp.float32)
        normed_ref[...] = modulated(xf, mod_ref[0:1, :], mod_ref[1:2, :]).astype(jnp.bfloat16)

    proj = jnp.dot(normed_ref[...], w_ref[...], preferred_element_type=jnp.float32)
    for low in range(0, BLOCK, LANES):
        part = proj[:, low : low + LANES]
        col = step * BLOCK + low + lax.broadcasted_iota(jnp.int32, (1, LANES), 1)
        factor = lax.rsqrt(head_means(part * part) + eps_norm)
        scaled = part * factor * jnp.where(col < n_query, gain_ref[...], 1.0)
        out_ref[:, low : low + LANES] = jnp.where(col < n_query + n_key, scaled, part).astype(
            jnp.bfloat16
        )


def picked(array, lead, shape, index):
    return pl.BlockSpec(
        (None,) * len(lead) + shape, lambda *grid: tuple(lead) + tuple(index(*grid))
    )


def qkv(x, x_lead, modulation, r, gain, w, n_query, n_key):
    rows, depth = x.shape[-2:]
    columns = w.shape[1]
    gain_row = jnp.tile(gain / math.sqrt(HEAD), LANES // HEAD)[None]
    return pl.pallas_call(
        functools.partial(qkv_kernel, n_query, n_key),
        grid=(pl.cdiv(columns, BLOCK),),
        in_specs=[
            picked(x, x_lead, (rows, depth), lambda i: (0, 0)),
            picked(modulation, (0, r), (3, depth), lambda i: (0, 0)),
            pl.BlockSpec((1, LANES), lambda i: (0, 0)),
            pl.BlockSpec((depth, BLOCK), lambda i: (0, i)),
        ],
        out_specs=pl.BlockSpec((rows, BLOCK), lambda i: (0, i)),
        out_shape=jax.ShapeDtypeStruct((rows, columns), jnp.bfloat16),
        scratch_shapes=[pltpu.VMEM((rows, depth), jnp.bfloat16)],
        compiler_params=PARAMS,
        cost_estimate=pl.CostEstimate(
            flops=2 * rows * depth * columns,
            bytes_accessed=2 * (depth * columns + rows * depth + rows * columns),
            transcendentals=0,
        ),
    )(x, modulation, gain_row, w)


def attend_kernel(n_sets, *refs):
    q_ref, out_ref = refs[0], refs[-1]
    sets = [refs[1 + 3 * s : 4 + 3 * s] for s in range(n_sets)]
    query = q_ref[...]
    rows = query.shape[0]
    lane = lax.broadcasted_iota(jnp.int32, (1, LANES), 1)
    low = lane < HEAD
    none = jnp.zeros((), jnp.bfloat16)
    one = jnp.ones((), jnp.bfloat16)
    both = jnp.concatenate([jnp.where(low, query, none), jnp.where(low, none, query)], 0)
    def scores_of(keys):
        return lax.dot_general(
            both, keys[...], (((1,), (1,)), ((), ())), preferred_element_type=jnp.float32
        )

    total = None
    scores = scores_of(sets[0][0])
    for place, (_, value_even, value_odd) in enumerate(sets):
        ahead = scores_of(sets[place + 1][0]) if place + 1 < len(sets) else None
        weights = jnp.exp(scores).astype(jnp.bfloat16)
        held = jnp.concatenate(
            [jnp.where(low, one, value_even[...]), jnp.where(low, value_odd[...], one)], 1
        )
        part = jnp.dot(weights, held, preferred_element_type=jnp.float32)
        total = part if total is None else total + part
        scores = ahead
    even, odd = total[:rows, :LANES], total[rows:, LANES:]
    halves = [pltpu.roll(each, HEAD, 1) / each for each in (even, odd)]
    out_ref[...] = jnp.where(lane < HEAD, halves[0], halves[1]).astype(jnp.bfloat16)


def attend(qkv_out, held_lead, n_query, sets, width):
    rows = qkv_out.shape[-2]
    pairs = n_query // LANES
    own = n_query // LANES
    last = 2 * width // LANES - 1
    first_value = width // LANES

    def specs(array, lead, offset):
        shape = (array.shape[-2], LANES)
        return [
            picked(array, lead, shape, lambda i: (0, offset + i)),
            picked(array, lead, shape, lambda i: (0, offset + first_value + i)),
            picked(
                array,
                lead,
                shape,
                lambda i: (0, offset + jnp.minimum(first_value + 1 + i, last)),
            ),
        ]

    in_specs = [picked(qkv_out, held_lead, (rows, LANES), lambda i: (0, i))]
    operands = [qkv_out]
    for array, lead, offset in [(qkv_out, held_lead, own)] + [pair + (0,) for pair in sets]:
        in_specs += specs(array, lead, offset)
        operands += [array] * 3
    count = rows + sum(array.shape[-2] for array, _ in sets)
    return pl.pallas_call(
        functools.partial(attend_kernel, 1 + len(sets)),
        grid=(pairs,),
        in_specs=in_specs,
        out_specs=pl.BlockSpec((rows, LANES), lambda i: (0, i)),
        out_shape=jax.ShapeDtypeStruct((rows, n_query), jnp.bfloat16),
        compiler_params=PARAMS,
        cost_estimate=pl.CostEstimate(
            flops=16 * rows * count * width,
            bytes_accessed=4 * count * width,
            transcendentals=rows * count * width // HEAD,
        ),
    )(*operands)


def out_kernel(width, x_ref, attn_ref, mod_ref, w_ref, *rest):
    attn = attn_ref[:, :width]
    proj = jnp.concatenate(
        [
            jnp.dot(attn, w_ref[shard], preferred_element_type=jnp.float32)
            for shard in range(w_ref.shape[0])
        ],
        -1,
    )
    x_next = (x_ref[...].astype(jnp.float32) + mod_ref[2:3, :] * proj).astype(jnp.bfloat16)
    if len(rest) == 1:
        rest[0][...] = x_next
        return
    fmod_ref, fw_ref, vel_ref = rest
    final = modulated(x_next.astype(jnp.float32), fmod_ref[0:1, :], fmod_ref[1:2, :])
    vel_ref[...] = jnp.dot(
        final.astype(jnp.bfloat16), fw_ref[...], preferred_element_type=jnp.float32
    )


def project_out(x, x_lead, attn, modulation, r, w, final=None):
    rows, depth = x.shape[-2:]
    width = w.shape[1]
    operands = [x, attn, modulation, w]
    specs = [
        picked(x, x_lead, (rows, depth), lambda i: (0, 0)),
        pl.BlockSpec(attn.shape, lambda i: (0, 0)),
        picked(modulation, (0, r), (3, depth), lambda i: (0, 0)),
        pl.BlockSpec(w.shape, lambda i: (0, 0, 0)),
    ]
    if final is None:
        shape = jax.ShapeDtypeStruct((rows, depth), jnp.bfloat16)
    else:
        operands += list(final)
        specs.append(picked(final[0], (r,), final[0].shape[1:], lambda i: (0, 0)))
        specs.append(pl.BlockSpec(final[1].shape, lambda i: (0, 0)))
        shape = jax.ShapeDtypeStruct((rows, final[1].shape[1]), jnp.float32)
    return pl.pallas_call(
        functools.partial(out_kernel, width),
        grid=(1,),
        in_specs=specs,
        out_specs=pl.BlockSpec(shape.shape, lambda i: (0, 0)),
        out_shape=shape,
        compiler_params=PARAMS,
        cost_estimate=pl.CostEstimate(
            flops=2 * rows * depth * width,
            bytes_accessed=2 * (depth * width + 3 * rows * depth),
            transcendentals=0,
        ),
    )(*operands)


MESH = pl.DeviceIdType.MESH


def greet(n, me, patch):
    has_left, has_right = me > 0, me < n - 1
    barrier = pltpu.get_barrier_semaphore()
    for other in (1, 2):
        pl.semaphore_signal(
            barrier, inc=1, device_id={"patch": patch ^ other}, device_id_type=MESH
        )

    @pl.when(has_left)
    def _():
        pl.semaphore_signal(barrier, inc=1, device_id={"shard": me - 1}, device_id_type=MESH)

    @pl.when(has_right)
    def _():
        pl.semaphore_signal(barrier, inc=1, device_id={"shard": me + 1}, device_id_type=MESH)

    pl.semaphore_wait(
        barrier, 2 + jnp.where(has_left, 1, 0) + jnp.where(has_right, 1, 0)
    )


def shard_block(me, way, t):
    return me - t if way == 0 else me + t


def relay(w_ref, spot, zs, zr, hs, hr):
    me = lax.axis_index("shard")
    patch = lax.axis_index("patch")

    def z_copy(way, t, k, sending):
        b = shard_block(me, way, t if sending else t + 1)
        dst = spot(None, b, patch, k)
        src = spot(w_ref, None, patch, k) if sending and t == 0 else dst
        return pltpu.make_async_remote_copy(
            src_ref=src,
            dst_ref=dst,
            send_sem=zs.at[way, t, k],
            recv_sem=zr.at[way, t, k],
            device_id={"shard": me + 1 if way == 0 else me - 1},
            device_id_type=MESH,
        )

    def hop(kind, way, t, k, sending):
        to = 2 if kind == 0 else 1
        held = patch ^ 2 if kind == 2 else patch
        place = spot(None, shard_block(me, way, t + 1), held if sending else held ^ to, k)
        return pltpu.make_async_remote_copy(
            src_ref=place,
            dst_ref=place,
            send_sem=hs.at[kind, way, t, k],
            recv_sem=hr.at[kind, way, t, k],
            device_id={"patch": patch ^ to},
            device_id_type=MESH,
        )

    return z_copy, hop


class Gather:
    def __init__(self, n, pieces, z_copy, hop):
        self.n, self.pieces, self.z_copy, self.hop = n, pieces, z_copy, hop
        self.me = lax.axis_index("shard")
        self.items = [
            (way, t, k) for t in range(n - 1) for k in range(len(pieces)) for way in range(2)
        ]

    def incoming(self, way, t):
        return (self.me - 1 - t >= 0) if way == 0 else (self.me + 1 + t < self.n)

    def ahead(self, way):
        return self.me < self.n - 1 if way == 0 else self.me > 0

    def begin(self):
        for way in range(2):

            @pl.when(self.ahead(way))
            def _(way=way):
                for k in range(len(self.pieces)):
                    self.z_copy(way, 0, k, True).start()

    def arrive(self, way, t, k):
        @pl.when(self.incoming(way, t))
        def _():
            self.z_copy(way, t, k, False).wait_recv()
            if t + 1 < self.n - 1:

                @pl.when(self.ahead(way))
                def _():
                    self.z_copy(way, t + 1, k, True).start()

            if self.pieces[k][3]:
                self.hop(0, way, t, k, True).start()
            self.hop(1, way, t, k, True).start()

    def pass_on(self, way, t, k):
        if self.pieces[k][3]:

            @pl.when(self.incoming(way, t))
            def _():
                self.hop(0, way, t, k, False).wait_recv()
                self.hop(2, way, t, k, True).start()

    def finish(self):
        for way, t, k in self.items:
            kinds = (0, 1, 2) if self.pieces[k][3] else (1,)

            @pl.when(self.incoming(way, t))
            def _(way=way, t=t, k=k, kinds=kinds):
                for kind in kinds:
                    self.hop(kind, way, t, k, True).wait_send()
                for kind in kinds:
                    if kind:
                        self.hop(kind, way, t, k, False).wait_recv()

            sends = self.incoming(way, t - 1) if t > 0 else True

            @pl.when(jnp.logical_and(self.ahead(way), sends))
            def _(way=way, t=t, k=k):
                self.z_copy(way, t, k, True).wait_send()


def gather_kernel(n, wo_ref, stale_ref, wo_all, stale_all, own, zs, zr, hs, hr, ss, sr):
    me = lax.axis_index("shard")
    patch = lax.axis_index("patch")
    requests = stale_ref.shape[0]
    size = wo_ref.shape[0] // 4
    greet(n, me, patch)

    def spot(ref, shard, quarter, k):
        place = wo_all.at[shard] if ref is None else ref
        return place.at[pl.ds(pl.multiple_of(quarter * size, 16), size)]

    def s_copy(kind, r):
        return pltpu.make_async_remote_copy(
            src_ref=stale_all.at[0, r] if kind == 2 else stale_ref.at[r],
            dst_ref=stale_all.at[kind, r],
            send_sem=ss.at[kind, r],
            recv_sem=sr.at[kind, r],
            device_id={"patch": patch ^ (2 if kind == 0 else 1)},
            device_id_type=MESH,
        )

    steps = Gather(n, ((0, 0, size, True),), *relay(wo_ref, spot, zs, zr, hs, hr))
    steps.begin()
    s_copy(0, 0).start()
    for r in range(requests):
        s_copy(1, r).start()
    own_o = pltpu.make_async_copy(wo_ref, wo_all.at[me], own)
    own_o.start()
    for item in steps.items:
        steps.arrive(*item)
    for r in range(1, requests):
        s_copy(0, r).start()
    s_copy(0, 0).wait_recv()
    s_copy(2, 0).start()
    for item in steps.items:
        steps.pass_on(*item)
    for r in range(1, requests):
        s_copy(0, r).wait_recv()
        s_copy(2, r).start()
    steps.finish()
    for r in range(requests):
        for kind in range(3):
            s_copy(kind, r).wait_send()
        for kind in (1, 2):
            s_copy(kind, r).wait_recv()
    own_o.wait()


def gather(w_out, stale, n):
    anywhere = pl.BlockSpec(memory_space=pl.ANY)
    dma = pltpu.SemaphoreType.DMA
    requests = stale.shape[0]
    return pl.pallas_call(
        functools.partial(gather_kernel, n),
        in_specs=[anywhere] * 2,
        out_specs=[anywhere] * 2,
        out_shape=[
            jax.ShapeDtypeStruct((n,) + w_out.shape, w_out.dtype),
            jax.ShapeDtypeStruct((3,) + stale.shape, stale.dtype),
        ],
        scratch_shapes=[
            dma,
            dma((2, n - 1, 1)),
            dma((2, n - 1, 1)),
            dma((3, 2, n - 1, 1)),
            dma((3, 2, n - 1, 1)),
            dma((3, requests)),
            dma((3, requests)),
        ],
        compiler_params=pltpu.CompilerParams(
            collective_id=0, has_side_effects=True, vmem_limit_bytes=56 * 1024 * 1024
        ),
        cost_estimate=pl.CostEstimate(
            flops=0, bytes_accessed=200 * 1024 * 1024, transcendentals=0
        ),
    )(w_out, stale)


def on_device(
    hidden,
    text_kv,
    stale_kv,
    modulation,
    score_gain,
    qkv_weight,
    out_weight,
    final_mod,
    final_weight,
    latent,
    step_index,
):
    section = lax.axis_index("section")
    patch = lax.axis_index("patch")
    patches = lax.axis_size("patch")
    shards = lax.axis_size("shard")
    requests, rows, depth = hidden.shape
    width = out_weight.shape[1]
    n_query = pl.cdiv(width, LANES) * LANES

    w = qkv_weight[0]
    share = w.shape[0] // patches
    mine = lax.dynamic_slice_in_dim(w, patch * share, share, 0)
    packed = jnp.concatenate(
        [
            mine[:, :width],
            jnp.zeros((share, n_query - width), w.dtype),
            mine[:, width:],
        ],
        1,
    )
    w_qkv = lax.all_gather(packed, ("shard", "patch"), axis=0, tiled=True)
    w_out, stale = gather(out_weight[0], stale_kv[0], shards)

    def layer(r, x, x_lead, final=None):
        held = qkv(x, x_lead, modulation, r, score_gain[0], w_qkv, n_query, width)
        sets = [(stale, (i, r)) for i in range(3)] + [(text_kv, (0, r))]
        attn = attend(held, (), n_query, sets, width)
        return project_out(x, x_lead, attn, modulation, r, w_out, final), held

    hop = [(s, s + 1) for s in range(lax.axis_size("section") - 1)]
    arrived, velocity, firsts, lasts = [], [], [], []
    for r in range(requests):
        x_next, held = layer(r, hidden, (r,))
        firsts.append(held)
        arrived.append(lax.ppermute(x_next, "section", hop))
    arrived = [lax.optimization_barrier((x, x_next))[0] for x in arrived[:-1]] + arrived[-1:]
    for r in range(requests):
        x = arrived[r]
        if velocity:
            x = lax.optimization_barrier((x, velocity[-1]))[0]
        vel, held = layer(r, x, (), (final_mod, final_weight))
        lasts.append(held)
        velocity.append(vel)
    fresh = jnp.stack(
        [
            jnp.where(section == 0, early, late)[:, n_query : n_query + 2 * width]
            for early, late in zip(firsts, lasts)
        ]
    )
    velocity = jnp.stack(velocity)
    half = latent.shape[1]
    back = lax.ppermute(velocity[:, :half].astype(jnp.bfloat16), "section", [(1, 0)])
    velocity_mine = jnp.where(section == 0, back.astype(jnp.float32), velocity[:, half:])
    sig = sigma_of(step_index)[:, None, None]
    sig_next = sigma_of(step_index + 1)[:, None, None]
    latent_next = latent + (sig_next - sig) * velocity_mine
    denoised = latent - sig * velocity_mine
    return (fresh[None], latent_next, denoised)


def solution(mesh):
    in_specs = (
        P("shard", "patch", None),
        P("section", "shard", None, None),
        P("section", "shard", "patch", None),
        P("section", "shard", None, None),
        P("section", None),
        P("section", "shard", None),
        P("section", None, "shard"),
        P("shard", None, None),
        P(),
        P("shard", ("patch", "section"), None),
        P("shard"),
    )
    out_specs = (
        P("section", "shard", "patch", None),
        P("shard", ("patch", "section"), None),
        P("shard", ("patch", "section"), None),
    )
    return jax.shard_map(
        on_device, mesh=mesh, in_specs=in_specs, out_specs=out_specs, check_vma=False
    )
```
